128 devices in a mesh: ctx: 32 (over y, z, core), rows: 4 (over x).
Axes of the slice: x: 4, y: 4, z: 4, core: 2. Of those that a mesh axis runs over, the one named last changes fastest.
Arguments:
- queries: bfloat16 [256, 2, 8, 1024], P(('ctx', 'rows')), may hold values from -160 to 160
- new_keys: bfloat16 [256, 2, 8, 128], P(('ctx', 'rows')), may hold values from -6 to 6
- new_values: bfloat16 [256, 2, 8, 128], P(('ctx', 'rows')), may hold values from -6 to 6
- recent_keys: bfloat16 [256, 8, 256, 128], P(('ctx', 'rows')), may hold values from -6 to 6
- recent_values: bfloat16 [256, 8, 256, 128], P(('ctx', 'rows')), may hold values from -6 to 6
- page_keys: bfloat16 [8192, 8, 64, 128], P(('ctx', 'rows')), may hold values from -6 to 6
- page_values: bfloat16 [8192, 8, 64, 128], P(('ctx', 'rows')), may hold values from -6 to 6
- page_fill: int32 [8192], P(('ctx', 'rows')), may hold values from 1 to 64
- top_owner: int32 [256, 8, 8], P(('ctx', 'rows')), may hold values from 0 to 127, all different within a row; in each aligned block of 16 rows (0 to 15, 16 to 31, ..., all dimensions but the last counted through in order) at most 2 rows name the same one
- top_slot: int32 [256, 8, 8], P(('ctx', 'rows')), may hold values from 0 to 63
Outputs:
- attended: bfloat16 [256, 2, 8, 1024], P(('ctx', 'rows'))
The draws below stay inside these ranges and needn't reach their ends.
Inputs may be any that keep to these rules, and one draw needn't show every extreme that they name: `top_owner`: each row names 8 different devices for one key-value head; in the rows of one device (aligned blocks of 16 rows of the first two dimensions) no device is named more than 2 times.
All inputs are finite; a program needn't handle non-finite values.
Results may differ from the reference program's by a relative error of at most 0.009.
Values may be sent and summed in bfloat16 or wider, within the bound.
No kernel may reach another device: no remote copies, remote signals or barrier semaphores. Data moves between devices by JAX's collectives and lax.ppermute only.
A program may use at most 128 MiB of HBM per device.

```python
import math
import jax
import jax.numpy as jnp
import numpy as np
from jax import lax

KV = 8
HPK = 8
HD = 128
NEW = 2
PS = 64
TOPK = 8
RECENT = 256
SEQ_DEV = 2
PAGES_DEV = 64
ROWS = 256
POOL = 8192
CAP = 2
N_CTX = 32
N_ROWS = 4


def shared_keys(key):
    return jnp.clip(jax.random.normal(key, (ROWS, NEW, KV, HD), jnp.float32), -5.5, 5.5)


def draw_new_keys(key, part):
    base = shared_keys(key)
    return base.astype(jnp.bfloat16)


def draw_queries(key, part):
    key = jax.random.fold_in(key, 7)
    key_fresh = jax.random.fold_in(key, 0)
    fresh = jnp.clip(jax.random.normal(key_fresh, (ROWS, NEW, KV, HPK, HD), jnp.float32), -6.0, 6.0)
    return fresh.reshape(ROWS, NEW, KV, HPK * HD).astype(jnp.bfloat16)


def touch_ends(entries, stream_key, smallest, high):
    place = [jax.random.randint(jax.random.fold_in(stream_key, axis), (), 0, length) for axis, length in enumerate(entries.shape)]
    widest = entries.shape.index(max(entries.shape))
    neighbour = place[:widest] + [(place[widest] + 1) % entries.shape[widest]] + place[widest + 1:]
    return entries.at[tuple(place)].set(smallest).at[tuple(neighbour)].set(high)


def shard_levels(stream_key, extent, shards, least, largest):
    gain, own = 1.0, jax.random.fold_in(stream_key, 6)
    for dim, parts in shards:
        heights = jnp.exp(jax.random.uniform(jax.random.fold_in(own, dim), (parts,), jnp.float32, least / len(shards), largest / len(shards)))
        gain = gain * jnp.repeat(heights, extent[dim] // parts).reshape([-1 if axis == dim else 1 for axis in range(len(extent))])
    return gain


def assign_block(rng, own, number, rows, number_of, top, reach, lean):
    order = jax.random.permutation(rng, number_of)
    heavy_load, ordinary = shares(number_of, rows * top, reach, lean, True), shares(number_of, rows * top, reach, lean, False)
    places = jnp.arange(number_of)

    def named(lengths, rotation):
        used = int((lengths > 0).sum())
        fixed = max(1, used // 4)
        passed = fixed + (places - fixed + rotation * (used - fixed)) % max(1, number_of - fixed)
        return jnp.zeros((number_of,), jnp.int32).at[order[jnp.where(places < fixed, places, passed)]].set(jnp.asarray(lengths, jnp.int32))

    lengths = jnp.where(number % 4 == 0, named(heavy_load, number // 4), named(ordinary, number - number // 4 - 1))
    mixed = jax.random.permutation(jax.random.fold_in(own, 3), number_of)
    source_of, taker = mixed[0:number_of // 2 * 2:2], mixed[1:number_of // 2 * 2:2]
    room = jnp.minimum(lengths[source_of] - 1, reach - lengths[taker]) // 2
    room = jnp.where((source_of == order[0]) | (taker == order[0]) | (lengths[taker] == 0), 0, jnp.maximum(room, 0))
    passed = jax.random.randint(jax.random.fold_in(own, 4), (number_of // 2,), 0, 1 << 20) % (room + 1)
    lengths = lengths.at[source_of].add(-passed).at[taker].add(passed)
    labels = jnp.searchsorted(jnp.cumsum(lengths), jnp.arange(rows * top), side="right").astype(jnp.int32)
    table = labels.reshape(top, rows).T
    table = table[jax.random.permutation(jax.random.fold_in(own, 1), rows)]
    rotation = jax.random.randint(jax.random.fold_in(own, 2), (rows, 1), 0, top)
    return jnp.take_along_axis(table, (jnp.arange(top)[None, :] + rotation) % top, axis=1)


def shares(count, total, reach, skew, full):
    loads = [(1 << 20) // math.isqrt(rank ** skew) + 1 for rank in range(1, count + 1)]
    largest = reach if full else min(reach, max(-(-total // count), total * loads[0] // sum(loads)))
    least = 1 if total - largest >= count - 1 else 0
    holding, surplus = [largest] + [least] * (count - 1), total - largest - least * (count - 1)
    while surplus > 0:
        free = [i for i in range(1, count) if holding[i] < largest] or [i for i in range(1, count) if holding[i] < reach]
        whole, left = sum([loads[i] for i in free]), surplus
        for i in free:
            more = min(reach - holding[i], max(1, left * loads[i] // whole), surplus)
            holding[i] = holding[i] + more
            surplus = surplus - more
    return np.array(holding)


def centred(key, shape, scale, most, shards=(), held_as=jnp.bfloat16):
    values = scale * jax.random.normal(key, shape, jnp.float32)
    if shards:
        values = values * shard_levels(key, shape, shards, -0.22, 0.18)
    return jnp.clip(values, -most, most).astype(held_as)


def setup_inputs(seed: int = 0) -> dict:
    splits = jax.random.split(jax.random.key(seed), 11)
    queries = draw_queries(jax.random.fold_in(splits[10], 71), 0)
    new_keys = draw_new_keys(jax.random.fold_in(splits[10], 71), 0)
    new_values = centred(splits[2], (ROWS, NEW, KV, HD), 1.0, 6.0, ((0, 128),))
    recent_keys = centred(splits[3], (ROWS, KV, RECENT, HD), 1.0, 6.0, ((0, 128),))
    recent_values = centred(splits[4], (ROWS, KV, RECENT, HD), 1.0, 6.0, ((0, 128),))
    page_keys = centred(splits[5], (POOL, KV, PS, HD), 1.0, 6.0, ((0, 128),))
    page_values = centred(splits[6], (POOL, KV, PS, HD), 1.0, 6.0, ((0, 128),))
    page_fill = touch_ends(jax.random.randint(splits[7], (POOL,), 1, PS + 1), jax.random.fold_in(splits[7], 1), 1, PS).astype(jnp.int32)
    top_owner_keys = jax.random.split(jax.random.fold_in(splits[8], 1), ROWS * KV // (SEQ_DEV * KV))
    top_owner_turns = jax.random.permutation(jax.random.fold_in(splits[8], 3), ROWS * KV // (SEQ_DEV * KV))
    top_owner = jax.vmap(lambda own, number: assign_block(jax.random.fold_in(splits[8], 2), own, number, SEQ_DEV * KV, N_CTX * N_ROWS, TOPK, CAP, 2))(top_owner_keys, top_owner_turns).reshape((ROWS, KV, TOPK))
    top_slot = touch_ends(jax.random.randint(splits[9], (ROWS, KV, TOPK), 0, PAGES_DEV), jax.random.fold_in(splits[9], 1), 0, PAGES_DEV - 1).astype(jnp.int32)
    return {"queries": queries, "new_keys": new_keys, "new_values": new_values, "recent_keys": recent_keys, "recent_values": recent_values, "page_keys": page_keys, "page_values": page_values, "page_fill": page_fill, "top_owner": top_owner, "top_slot": top_slot}


SCORE_FLOOR = -1e30


def reference(queries, new_keys, new_values, recent_keys, recent_values, page_keys, page_values, page_fill, top_owner, top_slot):
    score_scale = HD ** -0.5
    listed_pages = top_owner * PAGES_DEV + top_slot
    head_index = jnp.arange(KV, dtype=jnp.int32)[:, None]
    token_index = jnp.arange(PS, dtype=jnp.int32)
    query_step = jnp.arange(NEW * HPK, dtype=jnp.int32) // HPK
    causal = jnp.arange(NEW, dtype=jnp.int32)[None, :] <= query_step[:, None]

    def attend_row(row_index):
        query_rows = queries[row_index].astype(jnp.float32).reshape(NEW, KV, HPK, HD)
        query_rows = jnp.transpose(query_rows, (1, 0, 2, 3)).reshape(KV, NEW * HPK, HD)
        chosen = listed_pages[row_index]
        page_k = page_keys[chosen, head_index].astype(jnp.float32).reshape(KV, TOPK * PS, HD)
        page_v = page_values[chosen, head_index].astype(jnp.float32).reshape(KV, TOPK * PS, HD)
        filled = page_fill[chosen]
        is_live = (token_index[None, None, :] < filled[:, :, None]).reshape(KV, 1, TOPK * PS)
        page_scores = jnp.einsum("gqd,gjd->gqj", query_rows, page_k) * score_scale
        page_scores = jnp.where(is_live, page_scores, SCORE_FLOOR)
        near_k = recent_keys[row_index].astype(jnp.float32)
        near_scores = jnp.einsum("gqd,gjd->gqj", query_rows, near_k) * score_scale
        fresh_k = jnp.transpose(new_keys[row_index].astype(jnp.float32), (1, 0, 2))
        fresh_scores = jnp.einsum("gqd,gjd->gqj", query_rows, fresh_k) * score_scale
        fresh_scores = jnp.where(causal[None], fresh_scores, SCORE_FLOOR)
        all_scores = jnp.concatenate([page_scores, near_scores, fresh_scores], axis=2)
        peak_score = jnp.max(all_scores, axis=2, keepdims=True)
        weights = jnp.exp(all_scores - peak_score)
        fresh_v = jnp.transpose(new_values[row_index].astype(jnp.float32), (1, 0, 2))
        all_values = jnp.concatenate([page_v, recent_values[row_index].astype(jnp.float32), fresh_v], axis=1)
        mixed = jnp.einsum("gqj,gjd->gqd", weights, all_values) / jnp.sum(weights, axis=2, keepdims=True)
        mixed = jnp.transpose(mixed.reshape(KV, NEW, HPK, HD), (1, 0, 2, 3)).reshape(NEW, KV, HPK * HD)
        return mixed.astype(jnp.bfloat16)

    return lax.map(attend_row, jnp.arange(ROWS, dtype=jnp.int32))
```

```python
import functools

import jax
import jax.numpy as jnp
from jax import lax
from jax.experimental import pallas as pl
from jax.experimental.pallas import tpu as pltpu
from jax.sharding import PartitionSpec as P

AXES = ("ctx", "rows")
FLOOR = -1e30
LANES = 128
SLOTS = 2
TILE = 16
SPAN = SLOTS * TILE + SLOTS
MIB = 1024 * 1024


def lane_iota(rows):
    return lax.broadcasted_iota(jnp.int32, (rows, LANES), 1)


def row_iota(rows):
    return lax.broadcasted_iota(jnp.int32, (rows, LANES), 0)


def load_tiles(queries, tiles):
    seqs, steps, kv, wide = queries.shape
    group = wide // LANES
    for s in range(seqs):
        for t in range(steps):
            for h in range(group):
                block = queries[s, t, :, h * LANES : (h + 1) * LANES]
                start = s * kv * TILE + t * group + h
                tiles[pl.ds(start, kv, stride=TILE), :] = block.astype(jnp.float32)


def pack_kernel(picks, owner, slot, queries, out, place, tiles, wide, count):
    devices = wide.shape[0] // SPAN
    kv = queries.shape[2]
    load_tiles(queries, tiles)
    wide[...] = jnp.zeros_like(wide)

    def clear(i, carry):
        count[i] = 0
        return carry

    lax.fori_loop(0, devices, clear, 0, unroll=16)
    lane = lane_iota(1)

    def fill_tile(tile, carry):
        block = tiles[pl.ds(pl.multiple_of(tile * TILE, TILE), TILE), :]
        head = lax.rem(tile, kv)
        for k in range(picks):
            item = tile * picks + k
            to = owner[item]
            used = count[to]
            count[to] = used + 1
            place[item] = to * SLOTS + used
            base = to * SPAN
            wide[pl.ds(base + used * TILE, TILE), :] = block
            code = jnp.where(lane < LANES // 2, slot[item], head).astype(jnp.float32)
            wide[pl.ds(base + SLOTS * TILE + used, 1), :] = code
        return carry

    lax.fori_loop(0, tiles.shape[0] // TILE, fill_tile, 0, unroll=2)
    out[...] = wide[...].astype(out.dtype)


def local_kernel(queries, new_keys, new_values, keys, values, mixed, level, tiles, fresh):
    seqs, steps, kv, wide = queries.shape
    group = wide // LANES
    recent = keys.shape[2]
    scale = LANES ** (-0.5)
    load_tiles(queries, tiles)
    news = seqs * steps * kv
    for s in range(seqs):
        for u in range(steps):
            at = (s * steps + u) * kv
            fresh[at : at + kv, :] = new_keys[s, u].astype(jnp.float32)
            fresh[news + at : news + at + kv, :] = new_values[s, u].astype(jnp.float32)
    fresh_keys = fresh[:news, :].astype(jnp.bfloat16)
    fresh_values = jnp.concatenate(
        [fresh[news:, :].astype(jnp.bfloat16), jnp.ones((news, LANES), jnp.bfloat16)], axis=1
    )
    ones = jnp.ones((recent, LANES), jnp.bfloat16)
    col = lax.broadcasted_iota(jnp.int32, (TILE, news), 1)
    step = lax.broadcasted_iota(jnp.int32, (TILE, news), 0) // group
    nt = (((1,), (1,)), ((), ()))
    for s in range(seqs):
        for g in range(kv):
            at = (s * kv + g) * TILE
            query = tiles[at : at + TILE, :].astype(jnp.bfloat16)
            near = lax.dot_general(query, keys[s, g], nt, preferred_element_type=jnp.float32) * scale
            late = lax.dot_general(query, fresh_keys, nt, preferred_element_type=jnp.float32) * scale
            first = s * steps * kv + g
            seen = (col >= first) & (col <= first + step * kv) & (lax.rem(col, kv) == g)
            late = jnp.where(seen, late, FLOOR)
            peak = jnp.maximum(
                jnp.max(near, axis=1, keepdims=True), jnp.max(late, axis=1, keepdims=True)
            )
            near_weights = jnp.exp(near - peak).astype(jnp.bfloat16)
            late_weights = jnp.exp(late - peak).astype(jnp.bfloat16)
            both = jnp.concatenate([values[s, g], ones], axis=1)
            total = lax.dot(near_weights, both, preferred_element_type=jnp.float32)
            total = total + lax.dot(late_weights, fresh_values, preferred_element_type=jnp.float32)
            weight = total[:, LANES:]
            mixed[at : at + TILE, :] = total[:, :LANES] / weight
            level[at : at + TILE, :] = peak + jnp.log(weight)


def read_codes(wide, codes):
    devices = wide.shape[0] // SPAN
    half = LANES // 2
    lane = lane_iota(1)
    rows = []
    heads = []
    for c in range(SLOTS):
        low = jnp.zeros((8, LANES), jnp.float32)
        high = jnp.zeros((8, LANES), jnp.float32)
        for j in range(devices // 8):
            start = j * 8 * SPAN + SLOTS * TILE + c
            block = wide[pl.ds(start, 8, stride=SPAN), :]
            mine = lax.rem(lane_iota(8), half) == lax.rem(row_iota(8) + j * 8, half)
            block = jnp.where(mine, block, 0.0)
            if j * 8 < half:
                low = low + block
            else:
                high = high + block
        low = jnp.sum(low, axis=0, keepdims=True)
        high = jnp.sum(high, axis=0, keepdims=True)
        rows.append(jnp.where(lane < half, low, pltpu.roll(high, half, 1)))
        heads.append(jnp.where(lane < half, pltpu.roll(low, half, 1), high))
    for i, row in enumerate(rows + heads):
        codes[i : i + 1, :] = row.astype(jnp.int32)


def answer_kernel(kv, fill, got, keys, values, out, wide, answer, codes_v, codes, sem):
    devices = wide.shape[0] // SPAN
    page = keys.shape[1]
    scale = LANES ** (-0.5)
    wide[...] = got[...].astype(jnp.float32)
    codes_v[...] = jnp.zeros_like(codes_v)
    read_codes(wide, codes_v)
    copy = pltpu.make_async_copy(codes_v, codes, sem)
    copy.start()
    copy.wait()
    nt = (((1,), (1,)), ((), ()))
    lane = lane_iota(TILE)
    row = row_iota(TILE)
    group = 4
    ones = jnp.ones((group * page, LANES), jnp.bfloat16)
    blank = jnp.zeros((TILE, LANES), jnp.float32)
    piece = lane // TILE
    mine = lax.rem(lane, TILE) == row

    def attend(step, carry):
        spots, fills, queries, page_keys, page_values = [], [], [], [], []
        for a in range(group):
            message = step * (group // SLOTS) + a // SLOTS
            c = a % SLOTS
            number = codes[c, message]
            where = number * kv + codes[SLOTS + c, message]
            spots.append((message * SPAN + c * TILE, message * SPAN + SLOTS * TILE + c))
            fills.append(fill[number])
            queries.append(wide[pl.ds(spots[a][0], TILE), :].astype(jnp.bfloat16))
            page_keys.append(keys[where])
            page_values.append(values[where])
        scores = lax.dot_general(
            jnp.concatenate(queries, axis=0),
            jnp.concatenate(page_keys, axis=0),
            nt,
            preferred_element_type=jnp.float32,
        )
        weights, peaks = [], []
        for a in range(group):
            column = a * page // LANES
            first = a * page % LANES
            part = scores[a * TILE : (a + 1) * TILE, column * LANES : (column + 1) * LANES] * scale
            live = (lane >= first) & (lane < first + fills[a])
            part = jnp.where(live, part, FLOOR)
            peak = jnp.max(part, axis=1, keepdims=True)
            part = jnp.exp(part - peak)
            peaks.append(peak)
            line = [blank] * (group * page // LANES)
            line[column] = part
            weights.append(jnp.concatenate(line, axis=1))
        weights = jnp.concatenate(weights, axis=0).astype(jnp.bfloat16)
        both = jnp.concatenate([jnp.concatenate(page_values, axis=0), ones], axis=1)
        total = lax.dot(weights, both, preferred_element_type=jnp.float32)
        for a in range(group):
            part = total[a * TILE : (a + 1) * TILE, :]
            weight = part[:, LANES:]
            answer[pl.ds(spots[a][0], TILE), :] = part[:, :LANES] / weight
            level = peaks[a] + jnp.log(weight)
            high = level.astype(jnp.bfloat16).astype(jnp.float32)
            rest = level - high
            middle = rest.astype(jnp.bfloat16).astype(jnp.float32)
            low = rest - middle
            side = jnp.where(piece == 0, high, jnp.where(piece == 1, middle, low))
            side = jnp.where(mine & (piece < 3), side, 0.0)
            answer[pl.ds(spots[a][1], 1), :] = jnp.sum(side, axis=0, keepdims=True)
        return carry

    lax.fori_loop(0, devices * SLOTS // group, attend, 0, unroll=2)
    out[...] = answer[...].astype(out.dtype)


def merge_kernel(picks, place, got, mixed, level, out, wide, merged):
    seqs, steps, kv, width = out.shape
    group = width // LANES
    wide[...] = got[...].astype(jnp.float32)
    lane = lane_iota(TILE)
    mine = (lax.rem(lane, TILE) == row_iota(TILE)) & (lane < 3 * TILE)
    ones = jnp.ones((LANES, LANES), jnp.bfloat16)

    def merge(tile, carry):
        at = pl.multiple_of(tile * TILE, TILE)
        sides, parts = [], []
        for k in range(picks):
            spot = place[tile * picks + k]
            message = spot // SLOTS
            c = lax.rem(spot, SLOTS)
            parts.append(wide[pl.ds(message * SPAN + c * TILE, TILE), :])
            side = wide[pl.ds(message * SPAN + SLOTS * TILE + c, 1), :]
            sides.append(jnp.where(mine, side, 0.0))
        sides = jnp.concatenate(sides, axis=0).astype(jnp.bfloat16)
        levels = lax.dot(sides, ones, preferred_element_type=jnp.float32)
        levels = [levels[k * TILE : (k + 1) * TILE, :] for k in range(picks)]
        levels.append(level[pl.ds(at, TILE), :])
        parts.append(mixed[pl.ds(at, TILE), :])
        top = functools.reduce(jnp.maximum, levels)
        shares = [jnp.exp(x - top) for x in levels]
        total = functools.reduce(jnp.add, [w * x for w, x in zip(shares, parts)])
        merged[pl.ds(at, TILE), :] = total / functools.reduce(jnp.add, shares)
        return carry

    lax.fori_loop(0, merged.shape[0] // TILE, merge, 0, unroll=2)
    for s in range(seqs):
        for t in range(steps):
            for h in range(group):
                start = s * kv * TILE + t * group + h
                block = merged[pl.ds(start, kv, stride=TILE), :]
                out[s, t, :, h * LANES : (h + 1) * LANES] = block.astype(out.dtype)


VMEM = pl.BlockSpec(memory_space=pltpu.VMEM)
SMEM = pl.BlockSpec(memory_space=pltpu.SMEM)


def params(limit):
    return pltpu.CompilerParams(vmem_limit_bytes=limit * MIB)


def exchange(messages, devices):
    boxed = messages.reshape(devices, SPAN // 2, 2, LANES)
    boxed = lax.all_to_all(boxed, AXES, split_axis=0, concat_axis=0, tiled=True)
    return boxed.reshape(devices * SPAN, LANES)


def on_device(
    queries,
    new_keys,
    new_values,
    recent_keys,
    recent_values,
    page_keys,
    page_values,
    page_fill,
    top_owner,
    top_slot,
):
    seqs, steps, kv, width = queries.shape
    picks = top_owner.shape[2]
    items = seqs * kv * picks
    devices = lax.axis_size(AXES)
    rows = devices * SPAN
    tile_rows = seqs * kv * TILE
    wide = pltpu.VMEM((rows, LANES), jnp.float32)
    tiles = pltpu.VMEM((tile_rows, LANES), jnp.float32)
    messages = jax.ShapeDtypeStruct((rows, LANES), jnp.bfloat16)

    asked, place = pl.pallas_call(
        functools.partial(pack_kernel, picks),
        out_shape=(messages, jax.ShapeDtypeStruct((items,), jnp.int32)),
        in_specs=[SMEM, SMEM, VMEM],
        out_specs=(VMEM, SMEM),
        scratch_shapes=[tiles, wide, pltpu.SMEM((devices,), jnp.int32)],
        compiler_params=params(16),
        name="pack",
    )(top_owner.reshape(items), top_slot.reshape(items), queries)
    asked = exchange(asked, devices)

    near = jax.ShapeDtypeStruct((tile_rows, LANES), jnp.float32)
    mixed, level = pl.pallas_call(
        local_kernel,
        out_shape=(near, near),
        in_specs=[VMEM] * 5,
        out_specs=(VMEM, VMEM),
        scratch_shapes=[tiles, pltpu.VMEM((2 * seqs * steps * kv, LANES), jnp.float32)],
        compiler_params=params(16),
        cost_estimate=pl.CostEstimate(flops=70_000_000, bytes_accessed=3_000_000, transcendentals=70_000),
        name="near",
    )(queries, new_keys, new_values, recent_keys, recent_values)

    pages = page_keys.shape[0] * kv
    pool = (pages, page_keys.shape[2], LANES)
    answers = pl.pallas_call(
        functools.partial(answer_kernel, kv),
        out_shape=messages,
        in_specs=[SMEM, VMEM, VMEM, VMEM],
        out_specs=VMEM,
        scratch_shapes=[
            wide,
            wide,
            pltpu.VMEM((8, LANES), jnp.int32),
            pltpu.SMEM((8, LANES), jnp.int32),
            pltpu.SemaphoreType.DMA,
        ],
        compiler_params=params(16),
        name="answer",
    )(
        page_fill,
        asked,
        pltpu.with_memory_space_constraint(page_keys.reshape(pool), pltpu.VMEM),
        pltpu.with_memory_space_constraint(page_values.reshape(pool), pltpu.VMEM),
    )
    answers = exchange(answers, devices)

    return pl.pallas_call(
        functools.partial(merge_kernel, picks),
        out_shape=jax.ShapeDtypeStruct(queries.shape, jnp.bfloat16),
        in_specs=[SMEM, VMEM, VMEM, VMEM],
        out_specs=VMEM,
        scratch_shapes=[wide, tiles],
        compiler_params=params(16),
        name="merge",
    )(place, answers, mixed, level)


def solution(mesh):
    split = P(AXES)
    return jax.shard_map(
        on_device,
        mesh=mesh,
        in_specs=(split,) * 10,
        out_specs=split,
        check_vma=False,
    )
```

```python
import functools

import jax
import jax.numpy as jnp
from jax import lax
from jax.experimental import pallas as pl
from jax.experimental.pallas import tpu as pltpu
from jax.sharding import PartitionSpec as P

AXES = ("ctx", "rows")
FLOOR = -1e30
LANES = 128
SLOTS = 2
TILE = 16
SPAN = SLOTS * TILE + SLOTS
PIECES = 3
MIB = 1024 * 1024


def lane_iota(rows):
    return lax.broadcasted_iota(jnp.int32, (rows, LANES), 1)


def row_iota(rows):
    return lax.broadcasted_iota(jnp.int32, (rows, LANES), 0)


def load_tiles(queries, tiles):
    seqs, steps, kv, wide = queries.shape
    group = wide // LANES
    for s in range(seqs):
        for t in range(steps):
            for h in range(group):
                block = queries[s, t, :, h * LANES : (h + 1) * LANES]
                start = s * kv * TILE + t * group + h
                tiles[pl.ds(start, kv, stride=TILE), :] = block.astype(jnp.float32)


def pack_kernel(owner_hbm, slot_hbm, queries_hbm, out, place, owner, slot, queries, tiles, wide, count, sems):
    devices = wide.shape[0] // SPAN
    seqs, kv, picks = owner.shape
    copies = [
        pltpu.make_async_copy(source, target, sems.at[i])
        for i, (source, target) in enumerate(
            ((owner_hbm, owner), (slot_hbm, slot), (queries_hbm, queries))
        )
    ]
    for copy in copies:
        copy.start()
    wide[...] = jnp.zeros_like(wide)
    for i in range(devices):
        count[i] = 0
    for copy in copies:
        copy.wait()
    load_tiles(queries, tiles)
    lane = lane_iota(1)

    def fill_tiles(s, g):
        tile = s * kv + g
        block = tiles[pl.ds(pl.multiple_of(tile * TILE, TILE), TILE), :]
        to = [owner[s, g, k] for k in range(picks)]
        used = [count[d] for d in to]
        for k in range(picks):
            count[to[k]] = used[k] + 1
        for k in range(picks):
            base = to[k] * SPAN
            place[tile * picks + k] = to[k] * SLOTS + used[k]
            wide[pl.ds(base + used[k] * TILE, TILE), :] = block
            code = jnp.where(lane < LANES // 2, slot[s, g, k] + 1, g).astype(jnp.float32)
            wide[pl.ds(base + SLOTS * TILE + used[k], 1), :] = code

    for s in range(seqs):
        for g in range(kv):
            fill_tiles(s, g)
    out[...] = wide[...].astype(out.dtype)


def local_kernel(
    queries,
    new_keys,
    new_values,
    keys,
    values,
    mixed,
    level,
    tiles,
    fresh,
):
    seqs, steps, kv, wide = queries.shape
    group = wide // LANES
    recent = keys.shape[2]
    scale = LANES ** (-0.5)
    load_tiles(queries, tiles)
    news = seqs * steps * kv
    for s in range(seqs):
        for u in range(steps):
            at = (s * steps + u) * kv
            fresh[at : at + kv, :] = new_keys[s, u].astype(jnp.float32)
            fresh[news + at : news + at + kv, :] = new_values[s, u].astype(jnp.float32)
    fresh_keys = fresh[:news, :].astype(jnp.bfloat16)
    fresh_values = jnp.concatenate(
        [fresh[news:, :].astype(jnp.bfloat16), jnp.ones((news, LANES), jnp.bfloat16)], axis=1
    )
    ones = jnp.ones((recent, LANES), jnp.bfloat16)
    col = lax.broadcasted_iota(jnp.int32, (TILE, news), 1)
    step = lax.broadcasted_iota(jnp.int32, (TILE, news), 0) // group
    nt = (((1,), (1,)), ((), ()))
    for s in range(seqs):
        for g in range(kv):
            at = (s * kv + g) * TILE
            query = tiles[at : at + TILE, :].astype(jnp.bfloat16)
            near = lax.dot_general(query, keys[s, g], nt, preferred_element_type=jnp.float32) * scale
            late = lax.dot_general(query, fresh_keys, nt, preferred_element_type=jnp.float32) * scale
            first = s * steps * kv + g
            seen = (col >= first) & (col <= first + step * kv) & (lax.rem(col, kv) == g)
            late = jnp.where(seen, late, FLOOR)
            peak = jnp.maximum(
                jnp.max(near, axis=1, keepdims=True), jnp.max(late, axis=1, keepdims=True)
            )
            near_weights = jnp.exp(near - peak).astype(jnp.bfloat16)
            late_weights = jnp.exp(late - peak).astype(jnp.bfloat16)
            both = jnp.concatenate([values[s, g], ones], axis=1)
            total = lax.dot(near_weights, both, preferred_element_type=jnp.float32)
            total = total + lax.dot(late_weights, fresh_values, preferred_element_type=jnp.float32)
            weight = total[:, LANES:]
            mixed[at : at + TILE, :] = total[:, :LANES]
            level[at : at + TILE, :LANES] = jnp.broadcast_to(peak, (TILE, LANES))
            level[at : at + TILE, LANES:] = weight


def read_codes(pages, wide, codes):
    devices = wide.shape[0] // SPAN
    half = LANES // 2
    lane = lane_iota(1)
    rows = []
    heads = []
    for c in range(SLOTS):
        low = jnp.zeros((8, LANES), jnp.float32)
        high = jnp.zeros((8, LANES), jnp.float32)
        for j in range(devices // 8):
            start = j * 8 * SPAN + SLOTS * TILE + c
            block = wide[pl.ds(start, 8, stride=SPAN), :]
            mine = lax.rem(lane_iota(8), half) == lax.rem(row_iota(8) + j * 8, half)
            block = jnp.where(mine, block, 0.0)
            if j * 8 < half:
                low = low + block
            else:
                high = high + block
        low = jnp.sum(low, axis=0, keepdims=True)
        high = jnp.sum(high, axis=0, keepdims=True)
        row = jnp.where(lane < half, low, pltpu.roll(high, half, 1)).astype(jnp.int32)
        head = jnp.where(lane < half, pltpu.roll(low, half, 1), high).astype(jnp.int32)
        rows.append(jnp.where(row == 0, lax.rem(lane, pages), row - 1))
        heads.append(jnp.where(row == 0, lane // pages + c * (LANES // pages), head))
    spare = [jnp.zeros_like(rows[0])] * (codes.shape[0] - 2 * SLOTS)
    codes[...] = jnp.concatenate(rows + heads + spare, axis=0)


def answer_kernel(
    kv,
    batch,
    ahead,
    fill,
    got,
    keys,
    values,
    unused,
    out,
    wide,
    answer,
    sides,
    near_keys,
    near_values,
    codes_v,
    codes,
    sem,
    key_sems,
    value_sems,
):
    devices = wide.shape[0] // SPAN
    page = keys.shape[1]
    scale = LANES ** (-0.5)
    wide[...] = got[...].astype(jnp.float32)
    read_codes(fill.shape[0], wide, codes_v)
    copy = pltpu.make_async_copy(codes_v, codes, sem)
    copy.start()
    copy.wait()
    nt = (((1,), (1,)), ((), ()))
    lane = lane_iota(TILE)
    mine = lax.rem(lane, TILE) == row_iota(TILE)
    front = lane < PIECES * TILE
    per_score, per_mix = 4, 2
    ones = jnp.ones((per_mix * page, LANES), jnp.bfloat16)
    rounds = devices * SLOTS // batch

    def pull(step):
        for a in range(batch):
            item = step * batch + a
            where = codes[item % SLOTS, item // SLOTS] * kv + codes[SLOTS + item % SLOTS, item // SLOTS]
            pltpu.make_async_copy(keys.at[where], near_keys.at[item], key_sems.at[step]).start()
            pltpu.make_async_copy(values.at[where], near_values.at[item], value_sems.at[step]).start()

    def attend(step):
        span = pl.ds(step * batch, batch)
        pltpu.make_async_copy(keys.at[pl.ds(0, batch)], near_keys.at[span], key_sems.at[step]).wait()
        pltpu.make_async_copy(values.at[pl.ds(0, batch)], near_values.at[span], value_sems.at[step]).wait()
        spots, rows, fills, queries = [], [], [], []
        for a in range(batch):
            item = step * batch + a
            message, c = item // SLOTS, item % SLOTS
            spots.append(message * SPAN + c * TILE)
            rows.append(c * devices + message)
            fills.append(fill[codes[c, message]])
            queries.append(wide[pl.ds(spots[a], TILE), :].astype(jnp.bfloat16))
        scores = []
        for b in range(0, batch, per_score):
            block = lax.dot_general(
                jnp.concatenate(queries[b : b + per_score], axis=0),
                near_keys[pl.ds(step * batch + b, per_score)].reshape(per_score * page, LANES),
                nt,
                preferred_element_type=jnp.float32,
            )
            for a in range(per_score):
                column = a * page // LANES * LANES
                scores.append(block[a * TILE : (a + 1) * TILE, column : column + LANES])
        peaks, weights = [], []
        for a in range(batch):
            first = a * page % LANES
            live = (lane >= first) & (lane < first + fills[a])
            part = jnp.where(live, scores[a], FLOOR)
            peak = jnp.max(part, axis=1, keepdims=True)
            peaks.append(peak * scale)
            weights.append(jnp.exp((part - peak) * scale))
        totals = []
        for b in range(0, batch, per_mix):
            mix = jnp.concatenate(weights[b : b + per_mix], axis=0).astype(jnp.bfloat16)
            both = jnp.concatenate([near_values[pl.ds(step * batch + b, per_mix)].reshape(per_mix * page, LANES), ones], axis=1)
            block = lax.dot(mix, both, preferred_element_type=jnp.float32)
            for a in range(per_mix):
                totals.append(block[a * TILE : (a + 1) * TILE, :])
        for a in range(batch):
            answer[pl.ds(spots[a], TILE), :] = totals[a][:, :LANES]
            side = jnp.where(front, peaks[a], totals[a][:, LANES:])
            side = jnp.where(mine, side, 0.0)
            sides[pl.ds(rows[a], 1), :] = jnp.sum(side, axis=0, keepdims=True)

    for step in range(ahead):
        pull(step)
    for step in range(rounds):
        if step + ahead < rounds:
            pull(step + ahead)
        attend(step)
    piece = lax.rem(lane_iota(8) // TILE, PIECES)
    for c in range(SLOTS):
        for j in range(devices // 8):
            value = sides[c * devices + j * 8 : c * devices + j * 8 + 8, :]
            high = value.astype(jnp.bfloat16).astype(jnp.float32)
            rest = value - high
            middle = rest.astype(jnp.bfloat16).astype(jnp.float32)
            value = jnp.where(piece == 0, high, jnp.where(piece == 1, middle, rest - middle))
            answer[pl.ds(j * 8 * SPAN + SLOTS * TILE + c, 8, stride=SPAN), :] = value
    out[...] = answer[...].astype(out.dtype)


def merge_kernel(picks, batch, place, got, mixed, level, out, wide, merged):
    seqs, steps, kv, width = out.shape
    group = width // LANES
    wide[...] = got[...].astype(jnp.float32)
    lane = lane_iota(TILE)
    mine = (lax.rem(lane, TILE) == row_iota(TILE)) & (lane < 2 * PIECES * TILE)
    source = lax.broadcasted_iota(jnp.int32, (LANES, 2 * LANES), 0) // (PIECES * TILE)
    target = lax.broadcasted_iota(jnp.int32, (LANES, 2 * LANES), 1) // LANES
    spread = (source == target).astype(jnp.float32).astype(jnp.bfloat16)

    def merge(step, carry):
        spots, sums = [], []
        for b in range(batch):
            sides = []
            for k in range(picks):
                spot = place[(step * batch + b) * picks + k]
                message = spot // SLOTS
                c = lax.rem(spot, SLOTS)
                spots.append(message * SPAN + c * TILE)
                side = wide[pl.ds(message * SPAN + SLOTS * TILE + c, 1), :]
                sides.append(jnp.where(mine, side, 0.0))
            sides = jnp.concatenate(sides, axis=0).astype(jnp.bfloat16)
            sums.append(lax.dot(sides, spread, preferred_element_type=jnp.float32))
        for b in range(batch):
            at = pl.multiple_of((step * batch + b) * TILE, TILE)
            rows = [sums[b][k * TILE : (k + 1) * TILE, :] for k in range(picks)]
            rows.append(level[pl.ds(at, TILE), :])
            parts = [wide[pl.ds(spots[b * picks + k], TILE), :] for k in range(picks)]
            parts.append(mixed[pl.ds(at, TILE), :])
            peak = functools.reduce(jnp.maximum, [x[:, :LANES] for x in rows])
            shares = [jnp.exp(x[:, :LANES] - peak) for x in rows]
            total = functools.reduce(jnp.add, [w * x for w, x in zip(shares, parts)])
            weight = functools.reduce(jnp.add, [w * x[:, LANES:] for w, x in zip(shares, rows)])
            merged[pl.ds(at, TILE), :] = total / weight
        return carry

    lax.fori_loop(0, seqs * kv // batch, merge, 0)
    for s in range(seqs):
        for t in range(steps):
            for h in range(group):
                start = s * kv * TILE + t * group + h
                block = merged[pl.ds(start, kv, stride=TILE), :]
                out[s, t, :, h * LANES : (h + 1) * LANES] = block.astype(out.dtype)


VMEM = pl.BlockSpec(memory_space=pltpu.VMEM)
SMEM = pl.BlockSpec(memory_space=pltpu.SMEM)
ANY = pl.BlockSpec(memory_space=pl.ANY)


def params(limit):
    return pltpu.CompilerParams(vmem_limit_bytes=limit * MIB)


def in_hbm(array):
    return pltpu.with_memory_space_constraint(array, pltpu.HBM)


def exchange(messages, devices):
    boxed = messages.reshape(devices, SPAN // 2, 2, LANES)
    boxed = lax.all_to_all(boxed, AXES, split_axis=0, concat_axis=0, tiled=True)
    return boxed.reshape(devices * SPAN, LANES)


def on_device(
    queries,
    new_keys,
    new_values,
    recent_keys,
    recent_values,
    page_keys,
    page_values,
    page_fill,
    top_owner,
    top_slot,
):
    seqs, steps, kv, width = queries.shape
    picks = top_owner.shape[2]
    items = seqs * kv * picks
    devices = lax.axis_size(AXES)
    rows = devices * SPAN
    tile_rows = seqs * kv * TILE
    wide = pltpu.VMEM((rows, LANES), jnp.float32)
    tiles = pltpu.VMEM((tile_rows, LANES), jnp.float32)
    messages = jax.ShapeDtypeStruct((rows, LANES), jnp.bfloat16)

    asked, place = pl.pallas_call(
        pack_kernel,
        out_shape=(messages, jax.ShapeDtypeStruct((items,), jnp.int32)),
        in_specs=[ANY, ANY, ANY],
        out_specs=(VMEM, SMEM),
        scratch_shapes=[
            pltpu.SMEM(top_owner.shape, jnp.int32),
            pltpu.SMEM(top_slot.shape, jnp.int32),
            pltpu.VMEM(queries.shape, queries.dtype),
            tiles,
            wide,
            pltpu.SMEM((devices,), jnp.int32),
            pltpu.SemaphoreType.DMA((3,)),
        ],
        compiler_params=params(16),
        name="pack",
    )(in_hbm(top_owner), in_hbm(top_slot), in_hbm(queries))
    asked = exchange(asked, devices)

    mixed, level = pl.pallas_call(
        local_kernel,
        out_shape=(
            jax.ShapeDtypeStruct((tile_rows, LANES), jnp.float32),
            jax.ShapeDtypeStruct((tile_rows, 2 * LANES), jnp.float32),
        ),
        in_specs=[VMEM] * 5,
        out_specs=(VMEM,) * 2,
        scratch_shapes=[
            tiles,
            pltpu.VMEM((2 * seqs * steps * kv, LANES), jnp.float32),
        ],
        compiler_params=params(16),
        cost_estimate=pl.CostEstimate(flops=70_000_000, bytes_accessed=3_000_000, transcendentals=70_000),
        name="near",
    )(
        queries,
        new_keys,
        new_values,
        recent_keys,
        recent_values,
    )

    pool = (page_keys.shape[0] * kv, page_keys.shape[2], LANES)
    slots, batch = SLOTS * devices, 64
    pages = pltpu.VMEM((slots,) + pool[1:], page_keys.dtype)
    answers = pl.pallas_call(
        functools.partial(answer_kernel, kv, batch, 2),
        out_shape=messages,
        in_specs=[SMEM, VMEM, ANY, ANY, ANY],
        out_specs=VMEM,
        scratch_shapes=[
            wide,
            wide,
            pltpu.VMEM((slots, LANES), jnp.float32),
            pages,
            pages,
            pltpu.VMEM((8, LANES), jnp.int32),
            pltpu.SMEM((8, LANES), jnp.int32),
            pltpu.SemaphoreType.DMA,
            pltpu.SemaphoreType.DMA((slots // batch,)),
            pltpu.SemaphoreType.DMA((slots // batch,)),
        ],
        compiler_params=params(24),
        name="answer",
    )(page_fill, asked, in_hbm(page_keys.reshape(pool)), in_hbm(page_values.reshape(pool)), level)
    answers = exchange(answers, devices)

    return pl.pallas_call(
        functools.partial(merge_kernel, picks, 4),
        out_shape=jax.ShapeDtypeStruct(queries.shape, jnp.bfloat16),
        in_specs=[SMEM, VMEM, VMEM, VMEM],
        out_specs=VMEM,
        scratch_shapes=[wide, tiles],
        compiler_params=params(16),
        name="merge",
    )(place, answers, mixed, level)


def solution(mesh):
    split = P(AXES)
    return jax.shard_map(
        on_device,
        mesh=mesh,
        in_specs=(split,) * 10,
        out_specs=split,
        check_vma=False,
    )
```

```python
import functools

import jax
import jax.numpy as jnp
from jax import lax
from jax.experimental import pallas as pl
from jax.experimental.pallas import tpu as pltpu
from jax.sharding import PartitionSpec as P

AXES = ("ctx", "rows")
FLOOR = -1e30
LANES = 128
SLOTS = 2
TILE = 16
SPAN = SLOTS * TILE + SLOTS
PIECES = 3
MIB = 1024 * 1024


def lane_iota(rows):
    return lax.broadcasted_iota(jnp.int32, (rows, LANES), 1)


def row_iota(rows):
    return lax.broadcasted_iota(jnp.int32, (rows, LANES), 0)


def load_tiles(queries, tiles):
    seqs, steps, kv, wide = queries.shape
    group = wide // LANES
    for s in range(seqs):
        for t in range(steps):
            for h in range(group):
                block = queries[s, t, :, h * LANES : (h + 1) * LANES]
                start = s * kv * TILE + t * group + h
                tiles[pl.ds(start, kv, stride=TILE), :] = block.astype(jnp.float32)


def pack_kernel(owner_hbm, slot_hbm, queries_hbm, out, owner, slot, queries, tiles, wide, narrow, count, sems):
    devices = wide.shape[0] // SPAN
    seqs, kv, picks = owner.shape
    copies = [
        pltpu.make_async_copy(source, target, sems.at[i])
        for i, (source, target) in enumerate(
            ((owner_hbm, owner), (slot_hbm, slot), (queries_hbm, queries))
        )
    ]
    for copy in copies:
        copy.start()
    wide[...] = jnp.zeros_like(wide)
    for i in range(devices):
        count[i] = 0
    for copy in copies:
        copy.wait()
    load_tiles(queries, tiles)
    lane = lane_iota(1)
    for s in range(seqs):
        for g in range(kv):
            tile = s * kv + g
            block = tiles[tile * TILE : (tile + 1) * TILE, :]
            to = [owner[s, g, k] for k in range(picks)]
            used = [count[d] for d in to]
            for k in range(picks):
                count[to[k]] = used[k] + 1
            for k in range(picks):
                base = to[k] * SPAN
                wide[pl.ds(base + used[k] * TILE, TILE), :] = block
                code = jnp.where(lane < LANES // 2, slot[s, g, k] + 1, g).astype(jnp.float32)
                wide[pl.ds(base + SLOTS * TILE + used[k], 1), :] = code
    parts = narrow.shape[0]
    rows = narrow.shape[1]
    copies = []
    for i in range(parts):
        narrow[i] = wide[i * rows : (i + 1) * rows, :].astype(narrow.dtype)
        copies.append(
            pltpu.make_async_copy(narrow.at[i], out.at[pl.ds(i * rows, rows)], sems.at[3 + i])
        )
        copies[-1].start()
    for copy in copies:
        copy.wait()


def place_items(owner, place, count):
    seqs, kv, picks = owner.shape
    for i in range(count.shape[0]):
        count[i] = 0
    for s in range(seqs):
        for g in range(kv):
            to = [owner[s, g, k] for k in range(picks)]
            used = [count[d] for d in to]
            for k in range(picks):
                count[to[k]] = used[k] + 1
                place[(s * kv + g) * picks + k] = to[k] * SLOTS + used[k]


def local_kernel(
    queries,
    new_keys,
    new_values,
    keys,
    values,
    owner_hbm,
    mixed,
    level,
    place,
    tiles,
    fresh,
    owner,
    count,
    sem,
):
    copy = pltpu.make_async_copy(owner_hbm, owner, sem)
    copy.start()
    seqs, steps, kv, wide = queries.shape
    group = wide // LANES
    recent = keys.shape[2]
    scale = LANES ** (-0.5)
    load_tiles(queries, tiles)
    news = seqs * steps * kv
    for s in range(seqs):
        for u in range(steps):
            at = (s * steps + u) * kv
            fresh[at : at + kv, :] = new_keys[s, u].astype(jnp.float32)
            fresh[news + at : news + at + kv, :] = new_values[s, u].astype(jnp.float32)
    fresh_keys = fresh[:news, :].astype(jnp.bfloat16)
    fresh_values = jnp.concatenate(
        [fresh[news:, :].astype(jnp.bfloat16), jnp.ones((news, LANES), jnp.bfloat16)], axis=1
    )
    ones = jnp.ones((recent, LANES), jnp.bfloat16)
    col = lax.broadcasted_iota(jnp.int32, (TILE, news), 1)
    step = lax.broadcasted_iota(jnp.int32, (TILE, news), 0) // group
    nt = (((1,), (1,)), ((), ()))
    for s in range(seqs):
        for g in range(kv):
            at = (s * kv + g) * TILE
            query = tiles[at : at + TILE, :].astype(jnp.bfloat16)
            near = lax.dot_general(query, keys[s, g], nt, preferred_element_type=jnp.float32) * scale
            late = lax.dot_general(query, fresh_keys, nt, preferred_element_type=jnp.float32) * scale
            first = s * steps * kv + g
            seen = (col >= first) & (col <= first + step * kv) & (lax.rem(col, kv) == g)
            late = jnp.where(seen, late, FLOOR)
            peak = jnp.maximum(
                jnp.max(near, axis=1, keepdims=True), jnp.max(late, axis=1, keepdims=True)
            )
            near_weights = jnp.exp(near - peak).astype(jnp.bfloat16)
            late_weights = jnp.exp(late - peak).astype(jnp.bfloat16)
            both = jnp.concatenate([values[s, g], ones], axis=1)
            total = lax.dot(near_weights, both, preferred_element_type=jnp.float32)
            total = total + lax.dot(late_weights, fresh_values, preferred_element_type=jnp.float32)
            weight = total[:, LANES:]
            mixed[at : at + TILE, :] = total[:, :LANES]
            level[at : at + TILE, :LANES] = jnp.broadcast_to(peak, (TILE, LANES))
            level[at : at + TILE, LANES:] = weight
    copy.wait()
    place_items(owner, place, count)


def read_codes(pages, got, codes):
    devices = got.shape[0] // SPAN
    half = LANES // 2
    lane = lane_iota(1)
    number = lax.rem(lane_iota(8), half)
    sums = [[jnp.zeros((1, LANES), jnp.float32)] * 2 for _ in range(SLOTS)]
    for k in range(8):
        at = k * SPAN + SLOTS * TILE
        low = at // TILE * TILE
        inside = (at - low) // 8 * 8
        part = [jnp.zeros((8, LANES), jnp.float32)] * 2
        for j in range(devices // 8):
            message = j * 8 + k
            block = got[j * 8 * SPAN + low : j * 8 * SPAN + low + TILE, :].astype(jnp.float32)
            block = jnp.where(number == message % half, block[inside : inside + 8, :], 0.0)
            part[message // half] = part[message // half] + block
        row = at - low - inside
        for c in range(SLOTS):
            for i in range(2):
                sums[c][i] = sums[c][i] + part[i][row + c : row + c + 1, :]
    rows = []
    heads = []
    for c in range(SLOTS):
        low, high = sums[c]
        row = jnp.where(lane < half, low, pltpu.roll(high, half, 1)).astype(jnp.int32)
        head = jnp.where(lane < half, pltpu.roll(low, half, 1), high).astype(jnp.int32)
        rows.append(jnp.where(row == 0, lax.rem(lane, pages), row - 1))
        heads.append(jnp.where(row == 0, lane // pages + c * (LANES // pages), head))
    spare = [jnp.zeros_like(rows[0])] * (codes.shape[0] - 2 * SLOTS)
    codes[...] = jnp.concatenate(rows + heads + spare, axis=0)


def answer_kernel(
    kv,
    batch,
    ahead,
    fill_hbm,
    got,
    keys,
    values,
    unused,
    out,
    wide,
    answer,
    sides,
    near_keys,
    near_values,
    codes_v,
    codes,
    fill,
    sems,
    key_sems,
    value_sems,
):
    devices = wide.shape[0] // SPAN
    page = keys.shape[1]
    scale = LANES ** (-0.5)
    fill_copy = pltpu.make_async_copy(fill_hbm, fill, sems.at[0])
    fill_copy.start()
    read_codes(fill.shape[0], got, codes_v)
    codes_copy = pltpu.make_async_copy(codes_v, codes, sems.at[1])
    codes_copy.start()
    wide[...] = got[...].astype(jnp.float32)
    fill_copy.wait()
    codes_copy.wait()
    nt = (((1,), (1,)), ((), ()))
    lane = lane_iota(TILE)
    mine = lax.rem(lane, TILE) == row_iota(TILE)
    front = lane < PIECES * TILE
    per_score, per_mix = 4, 2
    ones = jnp.ones((per_mix * page, LANES), jnp.bfloat16)
    rounds = devices * SLOTS // batch
    piece = lax.rem(lane_iota(8) // TILE, PIECES)

    def pull(step):
        for a in range(batch):
            item = step * batch + a
            where = codes[item % SLOTS, item // SLOTS] * kv + codes[SLOTS + item % SLOTS, item // SLOTS]
            pltpu.make_async_copy(keys.at[where], near_keys.at[item], key_sems.at[step]).start()
            pltpu.make_async_copy(values.at[where], near_values.at[item], value_sems.at[step]).start()

    def attend(step):
        span = pl.ds(step * batch, batch)
        pltpu.make_async_copy(keys.at[pl.ds(0, batch)], near_keys.at[span], key_sems.at[step]).wait()
        pltpu.make_async_copy(values.at[pl.ds(0, batch)], near_values.at[span], value_sems.at[step]).wait()
        spots, rows, fills, queries = [], [], [], []
        for a in range(batch):
            item = step * batch + a
            message, c = item // SLOTS, item % SLOTS
            spots.append(message * SPAN + c * TILE)
            rows.append(c * (batch // SLOTS) + a // SLOTS)
            fills.append(fill[codes[c, message]])
            queries.append(wide[pl.ds(spots[a], TILE), :].astype(jnp.bfloat16))
        scores = []
        for b in range(0, batch, per_score):
            block = lax.dot_general(
                jnp.concatenate(queries[b : b + per_score], axis=0),
                near_keys[pl.ds(step * batch + b, per_score)].reshape(per_score * page, LANES),
                nt,
                preferred_element_type=jnp.float32,
            )
            for a in range(per_score):
                column = a * page // LANES * LANES
                scores.append(block[a * TILE : (a + 1) * TILE, column : column + LANES])
        peaks, weights = [], []
        for a in range(batch):
            first = a * page % LANES
            live = (lane >= first) & (lane < first + fills[a])
            part = jnp.where(live, scores[a], FLOOR)
            peak = jnp.max(part, axis=1, keepdims=True)
            peaks.append(peak * scale)
            weights.append(jnp.exp((part - peak) * scale))
        totals = []
        for b in range(0, batch, per_mix):
            mix = jnp.concatenate(weights[b : b + per_mix], axis=0).astype(jnp.bfloat16)
            both = jnp.concatenate([near_values[pl.ds(step * batch + b, per_mix)].reshape(per_mix * page, LANES), ones], axis=1)
            block = lax.dot(mix, both, preferred_element_type=jnp.float32)
            for a in range(per_mix):
                totals.append(block[a * TILE : (a + 1) * TILE, :])
        for a in range(batch):
            answer[pl.ds(spots[a], TILE), :] = totals[a][:, :LANES]
            side = jnp.where(front, peaks[a], totals[a][:, LANES:])
            side = jnp.where(mine, side, 0.0)
            sides[pl.ds(rows[a], 1), :] = jnp.sum(side, axis=0, keepdims=True)
        for c in range(SLOTS):
            for j in range(0, batch // SLOTS, 8):
                first = c * (batch // SLOTS) + j
                value = sides[first : first + 8, :]
                high = value.astype(jnp.bfloat16).astype(jnp.float32)
                rest = value - high
                middle = rest.astype(jnp.bfloat16).astype(jnp.float32)
                value = jnp.where(piece == 0, high, jnp.where(piece == 1, middle, rest - middle))
                start = (step * (batch // SLOTS) + j) * SPAN + SLOTS * TILE + c
                answer[pl.ds(start, 8, stride=SPAN), :] = value
        span = pl.ds(step * (batch // SLOTS) * SPAN, batch // SLOTS * SPAN)
        out[span, :] = answer[span, :].astype(out.dtype)

    for step in range(ahead):
        pull(step)
    for step in range(rounds):
        if step + ahead < rounds:
            pull(step + ahead)
        attend(step)


def merge_kernel(picks, batch, place_hbm, got, mixed, level, out, wide, merged, place, sem):
    seqs, steps, kv, width = out.shape
    group = width // LANES
    copy = pltpu.make_async_copy(place_hbm, place, sem)
    copy.start()
    wide[...] = got[...].astype(jnp.float32)
    copy.wait()
    lane = lane_iota(TILE)
    mine = (lax.rem(lane, TILE) == row_iota(TILE)) & (lane < 2 * PIECES * TILE)
    source = lax.broadcasted_iota(jnp.int32, (LANES, 2 * LANES), 0) // (PIECES * TILE)
    target = lax.broadcasted_iota(jnp.int32, (LANES, 2 * LANES), 1) // LANES
    spread = (source == target).astype(jnp.float32).astype(jnp.bfloat16)

    def merge(step):
        spots, sums = [], []
        for b in range(batch):
            sides = []
            for k in range(picks):
                spot = place[(step * batch + b) * picks + k]
                message = spot // SLOTS
                c = lax.rem(spot, SLOTS)
                spots.append(message * SPAN + c * TILE)
                side = wide[pl.ds(message * SPAN + SLOTS * TILE + c, 1), :]
                sides.append(jnp.where(mine, side, 0.0))
            sides = jnp.concatenate(sides, axis=0).astype(jnp.bfloat16)
            sums.append(lax.dot(sides, spread, preferred_element_type=jnp.float32))
        for b in range(batch):
            at = (step * batch + b) * TILE
            rows = [sums[b][k * TILE : (k + 1) * TILE, :] for k in range(picks)]
            rows.append(level[pl.ds(at, TILE), :])
            parts = [wide[pl.ds(spots[b * picks + k], TILE), :] for k in range(picks)]
            parts.append(mixed[pl.ds(at, TILE), :])
            peak = functools.reduce(jnp.maximum, [x[:, :LANES] for x in rows])
            shares = [jnp.exp(x[:, :LANES] - peak) for x in rows]
            total = functools.reduce(jnp.add, [w * x for w, x in zip(shares, parts)])
            weight = functools.reduce(jnp.add, [w * x[:, LANES:] for w, x in zip(shares, rows)])
            merged[pl.ds(at, TILE), :] = total / weight

    for step in range(seqs * kv // batch):
        merge(step)
    for s in range(seqs):
        for t in range(steps):
            for h in range(group):
                start = s * kv * TILE + t * group + h
                block = merged[pl.ds(start, kv, stride=TILE), :]
                out[s, t, :, h * LANES : (h + 1) * LANES] = block.astype(out.dtype)


VMEM = pl.BlockSpec(memory_space=pltpu.VMEM)
SMEM = pl.BlockSpec(memory_space=pltpu.SMEM)
ANY = pl.BlockSpec(memory_space=pl.ANY)


def params(limit):
    return pltpu.CompilerParams(vmem_limit_bytes=limit * MIB)


def in_hbm(array):
    return pltpu.with_memory_space_constraint(array, pltpu.HBM)


def exchange(messages, devices):
    boxed = messages.reshape(devices, SPAN // 2, 2, LANES)
    boxed = lax.all_to_all(boxed, AXES, split_axis=0, concat_axis=0, tiled=True)
    return boxed.reshape(devices * SPAN, LANES)


def on_device(
    queries,
    new_keys,
    new_values,
    recent_keys,
    recent_values,
    page_keys,
    page_values,
    page_fill,
    top_owner,
    top_slot,
):
    seqs, steps, kv, width = queries.shape
    picks = top_owner.shape[2]
    items = seqs * kv * picks
    devices = lax.axis_size(AXES)
    rows = devices * SPAN
    tile_rows = seqs * kv * TILE
    wide = pltpu.VMEM((rows, LANES), jnp.float32)
    tiles = pltpu.VMEM((tile_rows, LANES), jnp.float32)
    messages = jax.ShapeDtypeStruct((rows, LANES), jnp.bfloat16)

    parts = 4
    asked = pl.pallas_call(
        pack_kernel,
        out_shape=pltpu.HBM(messages.shape, messages.dtype),
        in_specs=[ANY, ANY, ANY],
        out_specs=ANY,
        scratch_shapes=[
            pltpu.SMEM(top_owner.shape, jnp.int32),
            pltpu.SMEM(top_slot.shape, jnp.int32),
            pltpu.VMEM(queries.shape, queries.dtype),
            tiles,
            wide,
            pltpu.VMEM((parts, rows // parts, LANES), messages.dtype),
            pltpu.SMEM((devices,), jnp.int32),
            pltpu.SemaphoreType.DMA((3 + parts,)),
        ],
        compiler_params=params(16),
        name="pack",
    )(in_hbm(top_owner), in_hbm(top_slot), in_hbm(queries))
    asked = exchange(asked, devices)

    mixed, level, place = pl.pallas_call(
        local_kernel,
        out_shape=(
            jax.ShapeDtypeStruct((tile_rows, LANES), jnp.float32),
            jax.ShapeDtypeStruct((tile_rows, 2 * LANES), jnp.float32),
            jax.ShapeDtypeStruct((items,), jnp.int32),
        ),
        in_specs=[VMEM] * 5 + [ANY],
        out_specs=(VMEM, VMEM, SMEM),
        scratch_shapes=[
            tiles,
            pltpu.VMEM((2 * seqs * steps * kv, LANES), jnp.float32),
            pltpu.SMEM(top_owner.shape, jnp.int32),
            pltpu.SMEM((devices,), jnp.int32),
            pltpu.SemaphoreType.DMA,
        ],
        compiler_params=params(16),
        cost_estimate=pl.CostEstimate(flops=70_000_000, bytes_accessed=3_000_000, transcendentals=70_000),
        name="near",
    )(
        queries,
        new_keys,
        new_values,
        recent_keys,
        recent_values,
        in_hbm(top_owner),
    )

    pool = (page_keys.shape[0] * kv, page_keys.shape[2], LANES)
    slots, batch = SLOTS * devices, 64
    pages = pltpu.VMEM((slots,) + pool[1:], page_keys.dtype)
    answers = pl.pallas_call(
        functools.partial(answer_kernel, kv, batch, 2),
        out_shape=messages,
        in_specs=[ANY, VMEM, ANY, ANY, ANY],
        out_specs=VMEM,
        scratch_shapes=[
            wide,
            wide,
            pltpu.VMEM((batch, LANES), jnp.float32),
            pages,
            pages,
            pltpu.VMEM((8, LANES), jnp.int32),
            pltpu.SMEM((8, LANES), jnp.int32),
            pltpu.SMEM(page_fill.shape, jnp.int32),
            pltpu.SemaphoreType.DMA((2,)),
            pltpu.SemaphoreType.DMA((slots // batch,)),
            pltpu.SemaphoreType.DMA((slots // batch,)),
        ],
        compiler_params=params(24),
        name="answer",
    )(in_hbm(page_fill), asked, in_hbm(page_keys.reshape(pool)), in_hbm(page_values.reshape(pool)), level)
    answers = exchange(answers, devices)

    return pl.pallas_call(
        functools.partial(merge_kernel, picks, 8),
        out_shape=jax.ShapeDtypeStruct(queries.shape, jnp.bfloat16),
        in_specs=[ANY, VMEM, VMEM, VMEM],
        out_specs=VMEM,
        scratch_shapes=[
            wide,
            tiles,
            pltpu.SMEM((items,), jnp.int32),
            pltpu.SemaphoreType.DMA,
        ],
        compiler_params=params(16),
        name="merge",
    )(place, answers, mixed, level)


def solution(mesh):
    split = P(AXES)
    return jax.shard_map(
        on_device,
        mesh=mesh,
        in_specs=(split,) * 10,
        out_specs=split,
        check_vma=False,
    )
```

```python
import functools

import jax
import jax.numpy as jnp
from jax import lax
from jax.experimental import pallas as pl
from jax.experimental.pallas import tpu as pltpu
from jax.sharding import PartitionSpec as P

AXES = ("ctx", "rows")
FLOOR = -1e30
LANES = 128
SLOTS = 2
TILE = 16
SPAN = SLOTS * TILE + SLOTS
PIECES = 3
MIB = 1024 * 1024
LOG2E = 1.4426950408889634


def lane_iota(rows):
    return lax.broadcasted_iota(jnp.int32, (rows, LANES), 1)


def row_iota(rows):
    return lax.broadcasted_iota(jnp.int32, (rows, LANES), 0)


def load_tiles(queries, tiles):
    seqs, steps, kv, wide = queries.shape
    group = wide // LANES
    for s in range(seqs):
        for t in range(steps):
            for h in range(group):
                block = queries[s, t, :, h * LANES : (h + 1) * LANES]
                start = s * kv * TILE + t * group + h
                tiles[pl.ds(start, kv, stride=TILE), :] = block.astype(jnp.float32)


def pack_kernel(owner_hbm, slot_hbm, queries_hbm, out, owner, slot, queries, tiles, wide, count, sems):
    devices = wide.shape[0] // SPAN
    seqs, kv, picks = owner.shape
    copies = [
        pltpu.make_async_copy(source, target, sems.at[i])
        for i, (source, target) in enumerate(
            ((owner_hbm, owner), (slot_hbm, slot), (queries_hbm, queries))
        )
    ]
    for copy in copies:
        copy.start()
    wide[...] = jnp.zeros_like(wide)
    for i in range(devices):
        count[i] = 0
    for copy in copies:
        copy.wait()
    load_tiles(queries, tiles)
    lane = lane_iota(1)
    for s in range(seqs):
        for g in range(kv):
            tile = s * kv + g
            block = tiles[tile * TILE : (tile + 1) * TILE, :]
            to = [owner[s, g, k] for k in range(picks)]
            used = [count[d] for d in to]
            for k in range(picks):
                count[to[k]] = used[k] + 1
            for k in range(picks):
                base = to[k] * SPAN
                wide[pl.ds(base + used[k] * TILE, TILE), :] = block
                code = jnp.where(lane < LANES // 2, slot[s, g, k] + 1, g).astype(jnp.float32)
                wide[pl.ds(base + SLOTS * TILE + used[k], 1), :] = code
    out[...] = wide[...].astype(out.dtype)


def place_items(owner, place, count):
    seqs, kv, picks = owner.shape
    for i in range(count.shape[0]):
        count[i] = 0
    for s in range(seqs):
        for g in range(kv):
            to = [owner[s, g, k] for k in range(picks)]
            used = [count[d] for d in to]
            for k in range(picks):
                count[to[k]] = used[k] + 1
                place[(s * kv + g) * picks + k] = to[k] * SLOTS + used[k]


def near_weights(queries, new_keys, keys, tiles):
    seqs, steps, kv, width = queries.shape
    group = width // LANES
    scale = LANES ** (-0.5)
    load_tiles(queries, tiles)
    news = seqs * steps * kv
    fresh = [new_keys[s, u].astype(jnp.float32) for s in range(seqs) for u in range(steps)]
    fresh = jnp.concatenate(fresh, axis=0).astype(jnp.bfloat16)
    nt = (((1,), (1,)), ((), ()))
    col = lax.broadcasted_iota(jnp.int32, (TILE, news), 1)
    step = lax.broadcasted_iota(jnp.int32, (TILE, news), 0) // group
    rows = tiles[...].astype(jnp.bfloat16)
    late = lax.dot_general(rows, fresh, nt, preferred_element_type=jnp.float32)
    spots = [(s, g, (s * kv + g) * TILE) for s in range(seqs) for g in range(kv)]
    near = [
        lax.dot_general(rows[at : at + TILE, :], keys[s, g], nt, preferred_element_type=jnp.float32)
        for s, g, at in spots
    ]
    near_parts, late_parts, peaks = [], [], []
    for (s, g, at), block in zip(spots, near):
        first = s * steps * kv + g
        seen = (col >= first) & (col <= first + step * kv) & (lax.rem(col, kv) == g)
        tail = jnp.where(seen, late[at : at + TILE, :], FLOOR)
        peak = jnp.maximum(
            jnp.max(block, axis=1, keepdims=True), jnp.max(tail, axis=1, keepdims=True)
        )
        near_parts.append(jnp.exp2((block - peak) * (scale * LOG2E)).astype(jnp.bfloat16))
        late_parts.append(jnp.exp2((tail - peak) * (scale * LOG2E)))
        peaks.append(peak * scale)
    return near_parts, jnp.concatenate(late_parts, axis=0).astype(jnp.bfloat16), peaks


def near_sums(weights, new_values, values, mixed, level):
    near_parts, late_parts, peaks = weights
    seqs, steps, kv, _ = new_values.shape
    fresh = [new_values[s, u].astype(jnp.float32) for s in range(seqs) for u in range(steps)]
    fresh = jnp.concatenate(fresh, axis=0).astype(jnp.bfloat16)
    fresh = jnp.concatenate([fresh, jnp.ones_like(fresh)], axis=1)
    late = lax.dot(late_parts, fresh, preferred_element_type=jnp.float32)
    ones = jnp.ones(values.shape[2:], jnp.bfloat16)
    for s in range(seqs):
        for g in range(kv):
            tile = s * kv + g
            at = tile * TILE
            both = jnp.concatenate([values[s, g], ones], axis=1)
            total = lax.dot(near_parts[tile], both, preferred_element_type=jnp.float32)
            total = total + late[at : at + TILE, :]
            mixed[at : at + TILE, :] = total[:, :LANES]
            level[at : at + TILE, :LANES] = jnp.broadcast_to(peaks[tile], (TILE, LANES))
            level[at : at + TILE, LANES:] = total[:, LANES:]


def read_codes(pages, got, codes):
    devices = got.shape[0] // SPAN
    half = LANES // 2
    lane = lane_iota(1)
    number = lax.rem(lane_iota(8), half)
    sums = [[jnp.zeros((1, LANES), jnp.float32)] * 2 for _ in range(SLOTS)]
    for k in range(8):
        at = k * SPAN + SLOTS * TILE
        low = at // TILE * TILE
        inside = (at - low) // 8 * 8
        part = [jnp.zeros((8, LANES), jnp.float32)] * 2
        for j in range(devices // 8):
            message = j * 8 + k
            block = got[j * 8 * SPAN + low : j * 8 * SPAN + low + TILE, :].astype(jnp.float32)
            block = jnp.where(number == message % half, block[inside : inside + 8, :], 0.0)
            part[message // half] = part[message // half] + block
        row = at - low - inside
        for c in range(SLOTS):
            for i in range(2):
                sums[c][i] = sums[c][i] + part[i][row + c : row + c + 1, :]
    rows = []
    heads = []
    for c in range(SLOTS):
        low, high = sums[c]
        row = jnp.where(lane < half, low, pltpu.roll(high, half, 1)).astype(jnp.int32)
        head = jnp.where(lane < half, pltpu.roll(low, half, 1), high).astype(jnp.int32)
        rows.append(jnp.where(row == 0, lax.rem(lane, pages), row - 1))
        heads.append(jnp.where(row == 0, lane // pages + c * (LANES // pages), head))
    spare = [jnp.zeros_like(rows[0])] * (codes.shape[0] - 2 * SLOTS)
    codes[...] = jnp.concatenate(rows + heads + spare, axis=0)


def answer_kernel(
    kv,
    batch,
    ahead,
    fill_hbm,
    owner_hbm,
    got,
    keys,
    values,
    queries,
    new_keys,
    new_values,
    recent_keys,
    recent_values,
    out,
    mixed,
    level,
    place_hbm,
    tiles,
    wide,
    answer,
    sides,
    near_keys,
    near_values,
    codes_v,
    codes,
    fill,
    owner,
    count,
    place,
    sems,
    key_sems,
    value_sems,
):
    devices = wide.shape[0] // SPAN
    page = keys.shape[1]
    scale = LANES ** (-0.5)
    fill_copy = pltpu.make_async_copy(fill_hbm, fill, sems.at[0])
    fill_copy.start()
    owner_copy = pltpu.make_async_copy(owner_hbm, owner, sems.at[2])
    owner_copy.start()
    read_codes(fill.shape[0], got, codes_v)
    codes_copy = pltpu.make_async_copy(codes_v, codes, sems.at[1])
    codes_copy.start()
    wide[...] = got[...].astype(jnp.float32)
    near = near_weights(queries, new_keys, recent_keys, tiles)
    fill_copy.wait()
    codes_copy.wait()
    nt = (((1,), (1,)), ((), ()))
    lane = lane_iota(TILE)
    mine = lax.rem(lane, TILE) == row_iota(TILE)
    front = lane < PIECES * TILE
    per_score, per_mix = 4, 2
    ones = jnp.ones((per_mix * page, LANES), jnp.bfloat16)
    rounds = devices * SLOTS // batch
    piece = lax.rem(lane_iota(8) // TILE, PIECES)

    def pull(step):
        for a in range(batch):
            item = step * batch + a
            message, c = item // SLOTS, item % SLOTS
            where = codes[c, message] * kv + codes[SLOTS + c, message]
            pltpu.make_async_copy(keys.at[where], near_keys.at[item], key_sems.at[step]).start()
            pltpu.make_async_copy(values.at[where], near_values.at[item], value_sems.at[step]).start()

    def attend(step):
        span = pl.ds(step * batch, batch)
        pltpu.make_async_copy(keys.at[pl.ds(0, batch)], near_keys.at[span], key_sems.at[step]).wait()
        pltpu.make_async_copy(values.at[pl.ds(0, batch)], near_values.at[span], value_sems.at[step]).wait()
        spots, rows, fills, asking = [], [], [], []
        for a in range(batch):
            item = step * batch + a
            message, c = item // SLOTS, item % SLOTS
            spots.append(message * SPAN + c * TILE)
            rows.append(c * (batch // SLOTS) + a // SLOTS)
            fills.append(fill[codes[c, message]])
            asking.append(wide[pl.ds(spots[a], TILE), :].astype(jnp.bfloat16))
        scores = []
        for b in range(0, batch, per_score):
            block = lax.dot_general(
                jnp.concatenate(asking[b : b + per_score], axis=0),
                near_keys[pl.ds(step * batch + b, per_score)].reshape(per_score * page, LANES),
                nt,
                preferred_element_type=jnp.float32,
            )
            for a in range(per_score):
                column = a * page // LANES * LANES
                scores.append(block[a * TILE : (a + 1) * TILE, column : column + LANES])
        peaks, weights = [], []
        for a in range(batch):
            first = a * page % LANES
            live = (lane >= first) & (lane < first + fills[a])
            part = jnp.where(live, scores[a], FLOOR)
            peak = jnp.max(part, axis=1, keepdims=True)
            peaks.append(peak)
            weights.append(jnp.exp2((part - peak) * (scale * LOG2E)))
        totals = []
        for b in range(0, batch, per_mix):
            mix = jnp.concatenate(weights[b : b + per_mix], axis=0).astype(jnp.bfloat16)
            both = jnp.concatenate([near_values[pl.ds(step * batch + b, per_mix)].reshape(per_mix * page, LANES), ones], axis=1)
            block = lax.dot(mix, both, preferred_element_type=jnp.float32)
            for a in range(per_mix):
                totals.append(block[a * TILE : (a + 1) * TILE, :])
        for a in range(batch):
            answer[pl.ds(spots[a], TILE), :] = totals[a][:, :LANES]
            side = jnp.where(front, peaks[a], totals[a][:, LANES:])
            side = jnp.where(mine, side, 0.0)
            sides[pl.ds(rows[a], 1), :] = jnp.sum(side, axis=0, keepdims=True)
        for c in range(SLOTS):
            for j in range(0, batch // SLOTS, 8):
                first = c * (batch // SLOTS) + j
                value = sides[first : first + 8, :]
                value = jnp.where(front[:8], value * scale, value)
                high = value.astype(jnp.bfloat16).astype(jnp.float32)
                rest = value - high
                middle = rest.astype(jnp.bfloat16).astype(jnp.float32)
                value = jnp.where(piece == 0, high, jnp.where(piece == 1, middle, rest - middle))
                start = (step * (batch // SLOTS) + j) * SPAN + SLOTS * TILE + c
                answer[pl.ds(start, 8, stride=SPAN), :] = value
        span = pl.ds(step * (batch // SLOTS) * SPAN, batch // SLOTS * SPAN)
        out[span, :] = answer[span, :].astype(out.dtype)

    for step in range(ahead):
        pull(step)
    owner_copy.wait()
    near_sums(near, new_values, recent_values, mixed, level)
    place_items(owner, place, count)
    place_copy = pltpu.make_async_copy(place, place_hbm, sems.at[3])
    place_copy.start()
    for step in range(rounds):
        if step + ahead < rounds:
            pull(step + ahead)
        attend(step)
    place_copy.wait()


def merge_kernel(
    picks,
    batch,
    place_hbm,
    got,
    mixed,
    level,
    out,
    wide,
    merged,
    place,
    ready,
    sem,
    back_sems,
):
    seqs, steps, kv, width = out.shape
    group = width // LANES
    copy = pltpu.make_async_copy(place_hbm, place, sem)
    copy.start()
    wide[...] = got[...].astype(jnp.float32)
    copy.wait()
    lane = lane_iota(TILE)
    mine = (lax.rem(lane, TILE) == row_iota(TILE)) & (lane < 2 * PIECES * TILE)
    source = lax.broadcasted_iota(jnp.int32, (LANES, 2 * LANES), 0) // (PIECES * TILE)
    target = lax.broadcasted_iota(jnp.int32, (LANES, 2 * LANES), 1) // LANES
    spread = (source == target).astype(jnp.float32).astype(jnp.bfloat16)

    def merge(step):
        spots, sums = [], []
        for b in range(batch):
            sides = []
            for k in range(picks):
                spot = place[(step * batch + b) * picks + k]
                message = spot // SLOTS
                c = lax.rem(spot, SLOTS)
                spots.append(message * SPAN + c * TILE)
                side = wide[pl.ds(message * SPAN + SLOTS * TILE + c, 1), :]
                sides.append(jnp.where(mine, side, 0.0))
            sides = jnp.concatenate(sides, axis=0).astype(jnp.bfloat16)
            sums.append(lax.dot(sides, spread, preferred_element_type=jnp.float32))
        for b in range(batch):
            at = (step * batch + b) * TILE
            rows = [sums[b][k * TILE : (k + 1) * TILE, :] for k in range(picks)]
            rows.append(level[pl.ds(at, TILE), :])
            parts = [wide[pl.ds(spots[b * picks + k], TILE), :] for k in range(picks)]
            parts.append(mixed[pl.ds(at, TILE), :])
            peak = functools.reduce(jnp.maximum, [x[:, :LANES] for x in rows])
            shares = [jnp.exp(x[:, :LANES] - peak) for x in rows]
            total = functools.reduce(jnp.add, [w * x for w, x in zip(shares, parts)])
            weight = functools.reduce(jnp.add, [w * x[:, LANES:] for w, x in zip(shares, rows)])
            merged[pl.ds(at, TILE), :] = total / weight

    backs = []
    for s in range(seqs):
        for step in range(s * kv // batch, (s + 1) * kv // batch):
            merge(step)
        for t in range(steps):
            for h in range(group):
                start = s * kv * TILE + t * group + h
                block = merged[pl.ds(start, kv, stride=TILE), :]
                ready[s, t, :, h * LANES : (h + 1) * LANES] = block.astype(ready.dtype)
        backs.append(pltpu.make_async_copy(ready.at[s], out.at[s], back_sems.at[s]))
        backs[-1].start()
    for back in backs:
        back.wait()


VMEM = pl.BlockSpec(memory_space=pltpu.VMEM)
SMEM = pl.BlockSpec(memory_space=pltpu.SMEM)
ANY = pl.BlockSpec(memory_space=pl.ANY)


def params(limit):
    return pltpu.CompilerParams(vmem_limit_bytes=limit * MIB)


def in_hbm(array):
    return pltpu.with_memory_space_constraint(array, pltpu.HBM)


def exchange(messages, devices):
    boxed = messages.reshape(devices, SPAN // 2, 2, LANES)
    boxed = lax.all_to_all(boxed, AXES, split_axis=0, concat_axis=0, tiled=True)
    return boxed.reshape(devices * SPAN, LANES)


def on_device(
    queries,
    new_keys,
    new_values,
    recent_keys,
    recent_values,
    page_keys,
    page_values,
    page_fill,
    top_owner,
    top_slot,
):
    seqs, steps, kv, width = queries.shape
    picks = top_owner.shape[2]
    items = seqs * kv * picks
    devices = lax.axis_size(AXES)
    rows = devices * SPAN
    tile_rows = seqs * kv * TILE
    wide = pltpu.VMEM((rows, LANES), jnp.float32)
    tiles = pltpu.VMEM((tile_rows, LANES), jnp.float32)
    messages = jax.ShapeDtypeStruct((rows, LANES), jnp.bfloat16)

    asked = pl.pallas_call(
        pack_kernel,
        out_shape=messages,
        in_specs=[ANY, ANY, ANY],
        out_specs=VMEM,
        scratch_shapes=[
            pltpu.SMEM(top_owner.shape, jnp.int32),
            pltpu.SMEM(top_slot.shape, jnp.int32),
            pltpu.VMEM(queries.shape, queries.dtype),
            tiles,
            wide,
            pltpu.SMEM((devices,), jnp.int32),
            pltpu.SemaphoreType.DMA((3,)),
        ],
        compiler_params=params(16),
        name="pack",
    )(in_hbm(top_owner), in_hbm(top_slot), in_hbm(queries))
    asked = exchange(asked, devices)

    pool = (page_keys.shape[0] * kv, page_keys.shape[2], LANES)
    slots, batch = SLOTS * devices, 64
    pages = pltpu.VMEM((slots,) + pool[1:], page_keys.dtype)
    answers, mixed, level, place = pl.pallas_call(
        functools.partial(answer_kernel, kv, batch, 2),
        out_shape=(
            messages,
            jax.ShapeDtypeStruct((tile_rows, LANES), jnp.float32),
            jax.ShapeDtypeStruct((tile_rows, 2 * LANES), jnp.float32),
            pltpu.HBM((items,), jnp.int32),
        ),
        in_specs=[ANY, ANY, VMEM, ANY, ANY] + [VMEM] * 5,
        out_specs=(VMEM, VMEM, VMEM, ANY),
        scratch_shapes=[
            tiles,
            wide,
            wide,
            pltpu.VMEM((batch, LANES), jnp.float32),
            pages,
            pages,
            pltpu.VMEM((8, LANES), jnp.int32),
            pltpu.SMEM((8, LANES), jnp.int32),
            pltpu.SMEM(page_fill.shape, jnp.int32),
            pltpu.SMEM(top_owner.shape, jnp.int32),
            pltpu.SMEM((devices,), jnp.int32),
            pltpu.SMEM((items,), jnp.int32),
            pltpu.SemaphoreType.DMA((4,)),
            pltpu.SemaphoreType.DMA((slots // batch,)),
            pltpu.SemaphoreType.DMA((slots // batch,)),
        ],
        compiler_params=params(24),
        name="answer",
    )(
        in_hbm(page_fill),
        in_hbm(top_owner),
        asked,
        in_hbm(page_keys.reshape(pool)),
        in_hbm(page_values.reshape(pool)),
        queries,
        new_keys,
        new_values,
        recent_keys,
        recent_values,
    )
    answers = exchange(answers, devices)

    return pl.pallas_call(
        functools.partial(merge_kernel, picks, 8),
        out_shape=jax.ShapeDtypeStruct(queries.shape, jnp.bfloat16),
        in_specs=[ANY, VMEM, VMEM, VMEM],
        out_specs=ANY,
        scratch_shapes=[
            wide,
            tiles,
            pltpu.SMEM((items,), jnp.int32),
            pltpu.VMEM(queries.shape, jnp.bfloat16),
            pltpu.SemaphoreType.DMA,
            pltpu.SemaphoreType.DMA((seqs,)),
        ],
        compiler_params=params(16),
        name="merge",
    )(place, answers, mixed, level)


def solution(mesh):
    split = P(AXES)
    return jax.shard_map(
        on_device,
        mesh=mesh,
        in_specs=(split,) * 10,
        out_specs=split,
        check_vma=False,
    )
```

```python
import functools

import jax
import jax.numpy as jnp
from jax import lax
from jax.experimental import pallas as pl
from jax.experimental.pallas import tpu as pltpu
from jax.sharding import PartitionSpec as P

AXES = ("ctx", "rows")
FLOOR = -1e30
LANES = 128
SLOTS = 2
TILE = 16
SPAN = SLOTS * TILE + SLOTS
PIECES = 3
MIB = 1024 * 1024
LOG2E = 1.4426950408889634


def lane_iota(rows):
    return lax.broadcasted_iota(jnp.int32, (rows, LANES), 1)


def row_iota(rows):
    return lax.broadcasted_iota(jnp.int32, (rows, LANES), 0)


def load_tiles(queries, tiles):
    seqs, steps, kv, wide = queries.shape
    group = wide // LANES
    for s in range(seqs):
        for t in range(steps):
            for h in range(group):
                block = queries[s, t, :, h * LANES : (h + 1) * LANES]
                start = s * kv * TILE + t * group + h
                tiles[pl.ds(start, kv, stride=TILE), :] = block.astype(jnp.float32)


def pack_kernel(owner_hbm, slot_hbm, queries_hbm, out, owner, slot, queries, tiles, wide, count, sems):
    devices = wide.shape[0] // SPAN
    seqs, kv, picks = owner.shape
    copies = [
        pltpu.make_async_copy(source, target, sems.at[i])
        for i, (source, target) in enumerate(
            ((owner_hbm, owner), (slot_hbm, slot), (queries_hbm, queries))
        )
    ]
    for copy in copies:
        copy.start()
    wide[...] = jnp.zeros_like(wide)
    for i in range(devices):
        count[i] = 0
    for copy in copies:
        copy.wait()
    load_tiles(queries, tiles)
    lane = lane_iota(1)
    for s in range(seqs):
        for g in range(kv):
            tile = s * kv + g
            block = tiles[tile * TILE : (tile + 1) * TILE, :]
            to = [owner[s, g, k] for k in range(picks)]
            used = [count[d] for d in to]
            for k in range(picks):
                count[to[k]] = used[k] + 1
            for k in range(picks):
                base = to[k] * SPAN
                wide[pl.ds(base + used[k] * TILE, TILE), :] = block
                code = jnp.where(lane < LANES // 2, slot[s, g, k] + 1, g).astype(jnp.float32)
                wide[pl.ds(base + SLOTS * TILE + used[k], 1), :] = code
    out[...] = wide[...].astype(out.dtype)


def place_items(owner, place, count):
    seqs, kv, picks = owner.shape
    for i in range(count.shape[0]):
        count[i] = 0
    for s in range(seqs):
        for g in range(kv):
            to = [owner[s, g, k] for k in range(picks)]
            used = [count[d] for d in to]
            for k in range(picks):
                count[to[k]] = used[k] + 1
                place[(s * kv + g) * picks + k] = to[k] * SLOTS + used[k]


def near_weights(queries, new_keys, keys, tiles):
    seqs, steps, kv, width = queries.shape
    group = width // LANES
    scale = LANES ** (-0.5)
    load_tiles(queries, tiles)
    news = seqs * steps * kv
    fresh = [new_keys[s, u].astype(jnp.float32) for s in range(seqs) for u in range(steps)]
    fresh = jnp.concatenate(fresh, axis=0).astype(jnp.bfloat16)
    nt = (((1,), (1,)), ((), ()))
    col = lax.broadcasted_iota(jnp.int32, (TILE, news), 1)
    step = lax.broadcasted_iota(jnp.int32, (TILE, news), 0) // group
    rows = tiles[...].astype(jnp.bfloat16)
    late = lax.dot_general(rows, fresh, nt, preferred_element_type=jnp.float32)
    spots = [(s, g, (s * kv + g) * TILE) for s in range(seqs) for g in range(kv)]
    near = [
        lax.dot_general(rows[at : at + TILE, :], keys[s, g], nt, preferred_element_type=jnp.float32)
        for s, g, at in spots
    ]
    near_parts, late_parts, peaks = [], [], []
    for (s, g, at), block in zip(spots, near):
        first = s * steps * kv + g
        seen = (col >= first) & (col <= first + step * kv) & (lax.rem(col, kv) == g)
        tail = jnp.where(seen, late[at : at + TILE, :], FLOOR)
        peak = jnp.maximum(
            jnp.max(block, axis=1, keepdims=True), jnp.max(tail, axis=1, keepdims=True)
        )
        near_parts.append(jnp.exp2((block - peak) * (scale * LOG2E)).astype(jnp.bfloat16))
        late_parts.append(jnp.exp2((tail - peak) * (scale * LOG2E)))
        peaks.append(peak * scale)
    return near_parts, jnp.concatenate(late_parts, axis=0).astype(jnp.bfloat16), peaks


def near_sums(weights, new_values, values, mixed, level):
    near_parts, late_parts, peaks = weights
    seqs, steps, kv, _ = new_values.shape
    fresh = [new_values[s, u].astype(jnp.float32) for s in range(seqs) for u in range(steps)]
    fresh = jnp.concatenate(fresh, axis=0).astype(jnp.bfloat16)
    fresh = jnp.concatenate([fresh, jnp.ones_like(fresh)], axis=1)
    late = lax.dot(late_parts, fresh, preferred_element_type=jnp.float32)
    ones = jnp.ones(values.shape[2:], jnp.bfloat16)
    for s in range(seqs):
        for g in range(kv):
            tile = s * kv + g
            at = tile * TILE
            both = jnp.concatenate([values[s, g], ones], axis=1)
            total = lax.dot(near_parts[tile], both, preferred_element_type=jnp.float32)
            total = total + late[at : at + TILE, :]
            mixed[at : at + TILE, :] = total[:, :LANES]
            level[at : at + TILE, :LANES] = jnp.broadcast_to(peaks[tile], (TILE, LANES))
            level[at : at + TILE, LANES:] = total[:, LANES:]


def read_codes(pages, got, codes):
    devices = got.shape[0] // SPAN
    half = LANES // 2
    lane = lane_iota(1)
    number = lax.rem(lane_iota(8), half)
    sums = [[jnp.zeros((1, LANES), jnp.float32)] * 2 for _ in range(SLOTS)]
    for k in range(8):
        at = k * SPAN + SLOTS * TILE
        low = at // TILE * TILE
        inside = (at - low) // 8 * 8
        part = [jnp.zeros((8, LANES), jnp.float32)] * 2
        for j in range(devices // 8):
            message = j * 8 + k
            block = got[j * 8 * SPAN + low : j * 8 * SPAN + low + TILE, :].astype(jnp.float32)
            block = jnp.where(number == message % half, block[inside : inside + 8, :], 0.0)
            part[message // half] = part[message // half] + block
        row = at - low - inside
        for c in range(SLOTS):
            for i in range(2):
                sums[c][i] = sums[c][i] + part[i][row + c : row + c + 1, :]
    rows = []
    heads = []
    for c in range(SLOTS):
        low, high = sums[c]
        row = jnp.where(lane < half, low, pltpu.roll(high, half, 1)).astype(jnp.int32)
        head = jnp.where(lane < half, pltpu.roll(low, half, 1), high).astype(jnp.int32)
        rows.append(jnp.where(row == 0, lax.rem(lane, pages), row - 1))
        heads.append(jnp.where(row == 0, lane // pages + c * (LANES // pages), head))
    spare = [jnp.zeros_like(rows[0])] * (codes.shape[0] - 2 * SLOTS)
    codes[...] = jnp.concatenate(rows + heads + spare, axis=0)


def answer_kernel(
    kv,
    batch,
    ahead,
    fill_hbm,
    owner_hbm,
    got,
    keys,
    values,
    queries,
    new_keys,
    new_values,
    recent_keys,
    recent_values,
    out,
    mixed,
    level,
    place_hbm,
    tiles,
    wide,
    answer,
    sides,
    near_keys,
    near_values,
    codes_v,
    codes,
    fill,
    owner,
    count,
    place,
    sems,
    key_sems,
    value_sems,
):
    devices = wide.shape[0] // SPAN
    page = keys.shape[1]
    scale = LANES ** (-0.5)
    fill_copy = pltpu.make_async_copy(fill_hbm, fill, sems.at[0])
    fill_copy.start()
    owner_copy = pltpu.make_async_copy(owner_hbm, owner, sems.at[2])
    owner_copy.start()
    read_codes(fill.shape[0], got, codes_v)
    codes_copy = pltpu.make_async_copy(codes_v, codes, sems.at[1])
    codes_copy.start()
    wide[...] = got[...].astype(jnp.float32)
    fill_copy.wait()
    codes_copy.wait()
    nt = (((1,), (1,)), ((), ()))
    lane = lane_iota(TILE)
    mine = lax.rem(lane, TILE) == row_iota(TILE)
    front = lane < PIECES * TILE
    per_score, per_mix = 4, 2
    ones = jnp.ones((per_mix * page, LANES), jnp.bfloat16)
    rounds = devices * SLOTS // batch
    lane8 = lane_iota(8)
    piece = lax.rem(lane_iota(8) // TILE, PIECES)

    def pull(step):
        for a in range(batch):
            item = step * batch + a
            message, c = item // SLOTS, item % SLOTS
            where = codes[c, message] * kv + codes[SLOTS + c, message]
            pltpu.make_async_copy(keys.at[where], near_keys.at[item], key_sems.at[step]).start()
            pltpu.make_async_copy(values.at[where], near_values.at[item], value_sems.at[step]).start()

    def attend(step):
        span = pl.ds(step * batch, batch)
        pltpu.make_async_copy(keys.at[pl.ds(0, batch)], near_keys.at[span], key_sems.at[step]).wait()
        pltpu.make_async_copy(values.at[pl.ds(0, batch)], near_values.at[span], value_sems.at[step]).wait()
        spots, rows, fills, asking = [], [], [], []
        for a in range(batch):
            item = step * batch + a
            message, c = item // SLOTS, item % SLOTS
            spots.append(message * SPAN + c * TILE)
            rows.append(c * (batch // SLOTS) + a // SLOTS)
            fills.append(fill[codes[c, message]])
            asking.append(wide[pl.ds(spots[a], TILE), :].astype(jnp.bfloat16))
        scores = []
        for b in range(0, batch, per_score):
            block = lax.dot_general(
                jnp.concatenate(asking[b : b + per_score], axis=0),
                near_keys[pl.ds(step * batch + b, per_score)].reshape(per_score * page, LANES),
                nt,
                preferred_element_type=jnp.float32,
            )
            for a in range(per_score):
                column = a * page // LANES * LANES
                scores.append(block[a * TILE : (a + 1) * TILE, column : column + LANES])
        peaks, weights = [], []
        for a in range(batch):
            first = a * page % LANES
            live = lane8 < first + fills[a]
            if first:
                live = live & (lane8 >= first)
            part = [jnp.where(live, scores[a][i : i + 8, :], FLOOR) for i in range(0, TILE, 8)]
            part = jnp.concatenate(part, axis=0)
            peak = jnp.max(part, axis=1, keepdims=True)
            peaks.append(peak)
            weights.append(jnp.exp2((part - peak) * (scale * LOG2E)))
        totals = []
        for b in range(0, batch, per_mix):
            mix = jnp.concatenate(weights[b : b + per_mix], axis=0).astype(jnp.bfloat16)
            both = jnp.concatenate([near_values[pl.ds(step * batch + b, per_mix)].reshape(per_mix * page, LANES), ones], axis=1)
            block = lax.dot(mix, both, preferred_element_type=jnp.float32)
            for a in range(per_mix):
                totals.append(block[a * TILE : (a + 1) * TILE, :])
        for a in range(batch):
            answer[pl.ds(spots[a], TILE), :] = totals[a][:, :LANES]
            side = jnp.where(front, peaks[a], totals[a][:, LANES:])
            side = jnp.where(mine, side, 0.0)
            sides[pl.ds(rows[a], 1), :] = jnp.sum(side, axis=0, keepdims=True)
        for c in range(SLOTS):
            for j in range(0, batch // SLOTS, 8):
                first = c * (batch // SLOTS) + j
                value = sides[first : first + 8, :]
                value = jnp.where(front[:8], value * scale, value)
                high = value.astype(jnp.bfloat16).astype(jnp.float32)
                rest = value - high
                middle = rest.astype(jnp.bfloat16).astype(jnp.float32)
                value = jnp.where(piece == 0, high, jnp.where(piece == 1, middle, rest - middle))
                start = (step * (batch // SLOTS) + j) * SPAN + SLOTS * TILE + c
                answer[pl.ds(start, 8, stride=SPAN), :] = value
        span = pl.ds(step * (batch // SLOTS) * SPAN, batch // SLOTS * SPAN)
        out[span, :] = answer[span, :].astype(out.dtype)

    for step in range(ahead):
        pull(step)
    near = near_weights(queries, new_keys, recent_keys, tiles)
    owner_copy.wait()
    near_sums(near, new_values, recent_values, mixed, level)
    place_items(owner, place, count)
    place_copy = pltpu.make_async_copy(place, place_hbm, sems.at[3])
    place_copy.start()
    for step in range(rounds):
        if step + ahead < rounds:
            pull(step + ahead)
        attend(step)
    place_copy.wait()


def merge_kernel(
    picks,
    batch,
    place_hbm,
    got,
    mixed,
    level,
    out,
    wide,
    merged,
    place,
    ready,
    sem,
    back_sems,
):
    seqs, steps, kv, width = out.shape
    group = width // LANES
    copy = pltpu.make_async_copy(place_hbm, place, sem)
    copy.start()
    wide[...] = got[...].astype(jnp.float32)
    copy.wait()
    lane = lane_iota(TILE)
    mine = (lax.rem(lane, TILE) == row_iota(TILE)) & (lane < 2 * PIECES * TILE)
    source = lax.broadcasted_iota(jnp.int32, (LANES, 2 * LANES), 0) // (PIECES * TILE)
    target = lax.broadcasted_iota(jnp.int32, (LANES, 2 * LANES), 1) // LANES
    spread = (source == target).astype(jnp.float32).astype(jnp.bfloat16)

    def merge(step):
        spots, sums = [], []
        for b in range(batch):
            sides = []
            for k in range(picks):
                spot = place[(step * batch + b) * picks + k]
                message = spot // SLOTS
                c = lax.rem(spot, SLOTS)
                spots.append(message * SPAN + c * TILE)
                side = wide[pl.ds(message * SPAN + SLOTS * TILE + c, 1), :]
                sides.append(jnp.where(mine, side, 0.0))
            sides = jnp.concatenate(sides, axis=0).astype(jnp.bfloat16)
            sums.append(lax.dot(sides, spread, preferred_element_type=jnp.float32))
        for b in range(batch):
            at = (step * batch + b) * TILE
            rows = [sums[b][k * TILE : (k + 1) * TILE, :] for k in range(picks)]
            rows.append(level[pl.ds(at, TILE), :])
            parts = [wide[pl.ds(spots[b * picks + k], TILE), :] for k in range(picks)]
            parts.append(mixed[pl.ds(at, TILE), :])
            peak = functools.reduce(jnp.maximum, [x[:, :LANES] for x in rows])
            shares = [jnp.exp(x[:, :LANES] - peak) for x in rows]
            total = functools.reduce(jnp.add, [w * x for w, x in zip(shares, parts)])
            weight = functools.reduce(jnp.add, [w * x[:, LANES:] for w, x in zip(shares, rows)])
            merged[pl.ds(at, TILE), :] = total / weight

    backs = []
    for s in range(seqs):
        for step in range(s * kv // batch, (s + 1) * kv // batch):
            merge(step)
        for t in range(steps):
            for h in range(group):
                start = s * kv * TILE + t * group + h
                block = merged[pl.ds(start, kv, stride=TILE), :]
                ready[s, t, :, h * LANES : (h + 1) * LANES] = block.astype(ready.dtype)
        backs.append(pltpu.make_async_copy(ready.at[s], out.at[s], back_sems.at[s]))
        backs[-1].start()
    for back in backs:
        back.wait()


VMEM = pl.BlockSpec(memory_space=pltpu.VMEM)
SMEM = pl.BlockSpec(memory_space=pltpu.SMEM)
ANY = pl.BlockSpec(memory_space=pl.ANY)


def params(limit):
    return pltpu.CompilerParams(vmem_limit_bytes=limit * MIB)


def in_hbm(array):
    return pltpu.with_memory_space_constraint(array, pltpu.HBM)


def exchange(messages, devices):
    boxed = messages.reshape(devices, SPAN // 2, 2, LANES)
    boxed = lax.all_to_all(boxed, AXES, split_axis=0, concat_axis=0, tiled=True)
    return boxed.reshape(devices * SPAN, LANES)


def on_device(
    queries,
    new_keys,
    new_values,
    recent_keys,
    recent_values,
    page_keys,
    page_values,
    page_fill,
    top_owner,
    top_slot,
):
    seqs, steps, kv, width = queries.shape
    picks = top_owner.shape[2]
    items = seqs * kv * picks
    devices = lax.axis_size(AXES)
    rows = devices * SPAN
    tile_rows = seqs * kv * TILE
    wide = pltpu.VMEM((rows, LANES), jnp.float32)
    tiles = pltpu.VMEM((tile_rows, LANES), jnp.float32)
    messages = jax.ShapeDtypeStruct((rows, LANES), jnp.bfloat16)

    asked = pl.pallas_call(
        pack_kernel,
        out_shape=messages,
        in_specs=[ANY, ANY, ANY],
        out_specs=VMEM,
        scratch_shapes=[
            pltpu.SMEM(top_owner.shape, jnp.int32),
            pltpu.SMEM(top_slot.shape, jnp.int32),
            pltpu.VMEM(queries.shape, queries.dtype),
            tiles,
            wide,
            pltpu.SMEM((devices,), jnp.int32),
            pltpu.SemaphoreType.DMA((3,)),
        ],
        compiler_params=params(16),
        name="pack",
    )(in_hbm(top_owner), in_hbm(top_slot), in_hbm(queries))
    asked = exchange(asked, devices)

    pool = (page_keys.shape[0] * kv, page_keys.shape[2], LANES)
    slots, batch = SLOTS * devices, 64
    pages = pltpu.VMEM((slots,) + pool[1:], page_keys.dtype)
    answers, mixed, level, place = pl.pallas_call(
        functools.partial(answer_kernel, kv, batch, 2),
        out_shape=(
            messages,
            jax.ShapeDtypeStruct((tile_rows, LANES), jnp.float32),
            jax.ShapeDtypeStruct((tile_rows, 2 * LANES), jnp.float32),
            pltpu.HBM((items,), jnp.int32),
        ),
        in_specs=[ANY, ANY, VMEM, ANY, ANY] + [VMEM] * 5,
        out_specs=(VMEM, VMEM, VMEM, ANY),
        scratch_shapes=[
            tiles,
            wide,
            wide,
            pltpu.VMEM((batch, LANES), jnp.float32),
            pages,
            pages,
            pltpu.VMEM((8, LANES), jnp.int32),
            pltpu.SMEM((8, LANES), jnp.int32),
            pltpu.SMEM(page_fill.shape, jnp.int32),
            pltpu.SMEM(top_owner.shape, jnp.int32),
            pltpu.SMEM((devices,), jnp.int32),
            pltpu.SMEM((items,), jnp.int32),
            pltpu.SemaphoreType.DMA((4,)),
            pltpu.SemaphoreType.DMA((slots // batch,)),
            pltpu.SemaphoreType.DMA((slots // batch,)),
        ],
        compiler_params=params(24),
        name="answer",
    )(
        in_hbm(page_fill),
        in_hbm(top_owner),
        asked,
        in_hbm(page_keys.reshape(pool)),
        in_hbm(page_values.reshape(pool)),
        queries,
        new_keys,
        new_values,
        recent_keys,
        recent_values,
    )
    answers = exchange(answers, devices)

    return pl.pallas_call(
        functools.partial(merge_kernel, picks, 4),
        out_shape=jax.ShapeDtypeStruct(queries.shape, jnp.bfloat16),
        in_specs=[ANY, VMEM, VMEM, VMEM],
        out_specs=ANY,
        scratch_shapes=[
            wide,
            tiles,
            pltpu.SMEM((items,), jnp.int32),
            pltpu.VMEM(queries.shape, jnp.bfloat16),
            pltpu.SemaphoreType.DMA,
            pltpu.SemaphoreType.DMA((seqs,)),
        ],
        compiler_params=params(16),
        name="merge",
    )(place, answers, mixed, level)


def solution(mesh):
    split = P(AXES)
    return jax.shard_map(
        on_device,
        mesh=mesh,
        in_specs=(split,) * 10,
        out_specs=split,
        check_vma=False,
    )
```
